128 devices in a mesh: row: 16 (over y_hi, z, core), col: 8 (over x, y_lo).
Axes of the slice: x: 4, y: 4 (y_hi: 2, y_lo: 2; y = y_hi * 2 + y_lo), z: 4, core: 2. Of those that a mesh axis runs over, the one named last changes fastest.
Arguments:
- features: bfloat16 [65536, 128], P('col', 'row'), may hold values from -6 to 6
- weight: bfloat16 [128, 128], replicated, may hold values from -0.5 to 0.5
- tiles: bfloat16 [16, 8, 256, 128, 128], P('row', 'col'), may hold values from 0 to 0.019897461
- tile_rows: int32 [16, 8, 256], P('row', 'col'), may hold values from 0 to 31, as said below
- tile_cols: int32 [16, 8, 256], P('row', 'col'), may hold values from 0 to 63
- tile_count: int32 [16, 8], P('row', 'col'), may hold values from 1 to 256, as said below
- cotangent: bfloat16 [65536, 128], P(('row', 'col')), may hold values from -6 to 6
Outputs:
- activated: bfloat16 [65536, 128], P(('row', 'col'))
- grad_weight: float32 [128, 128], P('row')
- grad_features: bfloat16 [65536, 128], P('col', 'row')
The draws below stay inside these ranges and needn't reach their ends.
Inputs may be any that keep to these rules, and one draw needn't show every extreme that they name: Within one grid cell the live and padded slots name distinct (tile_rows, tile_cols) pairs. `tile_count`: some grid cell is full in every draw.
All inputs are finite; a program needn't handle non-finite values.
Results may differ from the reference program's by a relative error of at most 0.006.
Values may be sent and summed in bfloat16 or wider, within the bound.
A program may use at most 128 MiB of HBM per device.

```python
import jax
import jax.numpy as jnp
from jax import lax

F = 128
BLK = 128
BR = 32
TILE_CAP = 256
BC = 64
GRID_R = 16
GRID_C = 8
NODES = 65536


def tile_positions(key):
    keys = jax.random.split(key, GRID_R * GRID_C)

    def one_cell(cell_key):
        return jax.random.permutation(cell_key, BR * BC)[:TILE_CAP].astype(jnp.int32)
    return jax.vmap(one_cell)(keys).reshape(GRID_R, GRID_C, TILE_CAP)


def draw_tile_rows(key, part):
    positions = tile_positions(key)
    return (positions // BC).astype(jnp.int32)


def draw_tile_cols(key, part):
    positions = tile_positions(key)
    return (positions % BC).astype(jnp.int32)


def draw_tile_count(key, part):
    key = jax.random.fold_in(key, 7)
    first, second = jax.random.split(key)
    shifts = jax.random.randint(first, (GRID_R * GRID_C,), 0, 4).astype(jnp.int32)
    chosen = jax.random.randint(second, (), 0, GRID_R * GRID_C).astype(jnp.int32)
    shifts = jnp.where(jnp.arange(GRID_R * GRID_C, dtype=jnp.int32) == chosen, 0, shifts)
    counts = jnp.maximum(1, jnp.right_shift(jnp.full((GRID_R * GRID_C,), TILE_CAP, jnp.int32), shifts))
    return counts.reshape(GRID_R, GRID_C).astype(jnp.int32)


def shard_levels(rng, dims, cuts, low, high):
    level = 1.0
    for dim, shards_of in cuts:
        draws = jax.random.uniform(jax.random.fold_in(jax.random.fold_in(rng, 6), dim), (shards_of,), jnp.float32, low / len(cuts), high / len(cuts))
        level = level * jnp.repeat(jnp.exp(draws), dims[dim] // shards_of).reshape((-1,) + (1,) * (len(dims) - 1 - dim))
    return level


def noise(stream_key, extent, width, reach, cuts=(), kind=jnp.bfloat16):
    loudness = shard_levels(stream_key, extent, cuts, -0.22, 0.18) if cuts else 1.0
    entries = jax.random.normal(stream_key, extent, jnp.float32) * width * loudness
    return jnp.minimum(jnp.maximum(entries, -reach), reach).astype(kind)


def setup_inputs(seed: int = 0) -> dict:
    seeds = jax.random.split(jax.random.key(seed), 8)
    return {
        "features": noise(seeds[0], (NODES, F), 1.0, 6.0, ((0, 8), (1, 16))),
        "weight": noise(seeds[1], (F, F), F ** -0.5, 0.5),
        "tiles": jnp.clip(0.019897461 * jax.random.uniform(seeds[2], (GRID_R, GRID_C, TILE_CAP, BLK, BLK), jnp.float32) ** shard_levels(seeds[2], (GRID_R, GRID_C, TILE_CAP, BLK, BLK), ((0, 16), (1, 8)), -0.2, 0.2), 0.0, 0.019897461).astype(jnp.bfloat16),
        "tile_rows": draw_tile_rows(jax.random.fold_in(seeds[7], 71), 0),
        "tile_cols": draw_tile_cols(jax.random.fold_in(seeds[7], 71), 0),
        "tile_count": draw_tile_count(jax.random.fold_in(seeds[7], 71), 0),
        "cotangent": noise(seeds[6], (NODES, F), 1.0, 6.0, ((0, 128),)),
    }


def reference(features, weight, tiles, tile_rows, tile_cols, tile_count, cotangent):
    hidden = jnp.dot(features, weight, preferred_element_type=jnp.float32).astype(jnp.bfloat16)
    nblocks = NODES // BLK
    hidden_blocks = hidden.reshape(nblocks, BLK, F)
    slots = jnp.arange(TILE_CAP, dtype=jnp.int32)

    def cell_info(index):
        rpos = index // GRID_C
        cpos = index % GRID_C
        tile_set = tiles[rpos, cpos].astype(jnp.float32)
        grows = (tile_rows[rpos, cpos] + rpos * BR).astype(jnp.int32)
        gcols = (tile_cols[rpos, cpos] + cpos * BC).astype(jnp.int32)
        live = slots < tile_count[rpos, cpos]
        return tile_set, grows, gcols, live

    def forward_cell(index, total):
        tile_set, grows, gcols, live = cell_info(index)
        picked = hidden_blocks[gcols].astype(jnp.float32)
        prods = jnp.einsum("tij,tjf->tif", tile_set, picked, precision=lax.Precision.HIGHEST)
        prods = jnp.where(live[:, None, None], prods, jnp.zeros_like(prods))
        return total.at[grows].add(prods)

    pre = lax.fori_loop(0, GRID_R * GRID_C, forward_cell, jnp.zeros((nblocks, BLK, F), jnp.float32)).reshape(NODES, F)
    sig = jax.nn.sigmoid(pre)
    activated = (pre * sig).astype(jnp.bfloat16)
    grad_pre = (cotangent.astype(jnp.float32) * sig * (1.0 + pre * (1.0 - sig))).astype(jnp.bfloat16)
    grad_blocks = grad_pre.reshape(nblocks, BLK, F)

    def backward_cell(index, total):
        tile_set, grows, gcols, live = cell_info(index)
        picked = grad_blocks[grows].astype(jnp.float32)
        prods = jnp.einsum("tji,tjf->tif", tile_set, picked, precision=lax.Precision.HIGHEST)
        prods = jnp.where(live[:, None, None], prods, jnp.zeros_like(prods))
        return total.at[gcols].add(prods)

    grad_hidden = lax.fori_loop(0, GRID_R * GRID_C, backward_cell, jnp.zeros((nblocks, BLK, F), jnp.float32))
    grad_hidden = grad_hidden.reshape(NODES, F).astype(jnp.bfloat16)
    grad_weight = jnp.dot(features.T, grad_hidden, preferred_element_type=jnp.float32)
    grad_features = jnp.dot(grad_hidden, weight.T, preferred_element_type=jnp.float32).astype(jnp.bfloat16)
    return activated, grad_weight, grad_features
```

```python
import functools

import jax
import jax.numpy as jnp
from jax import lax
from jax.experimental import pallas as pl
from jax.experimental.pallas import tpu as pltpu
from jax.sharding import PartitionSpec as P

F = 128
BLK = 128
NROW = 16
NCOL = 8
BR = 32
BC = 64
TILE_CAP = 256
CHUNK = 512
SUB = CHUNK // BLK
PER = F // NROW
STEP = 16
MIB = 1024 * 1024
MESH = pl.DeviceIdType.MESH
CHIPS = [(0, 1), (0, 3), (1, 0), (1, 1), (1, 3), (0, 2), (1, 2)]

f32 = jnp.float32
bf16 = jnp.bfloat16


def any_spec():
    return pl.BlockSpec(memory_space=pl.ANY)


def vmem_spec():
    return pl.BlockSpec(memory_space=pltpu.VMEM)


def greet(rows, cols):
    barrier = pltpu.get_barrier_semaphore()
    for r in rows:
        pl.semaphore_signal(barrier, inc=1, device_id={"row": r}, device_id_type=MESH)
    for c in cols:
        pl.semaphore_signal(barrier, inc=1, device_id={"col": c}, device_id_type=MESH)
    pl.semaphore_wait(barrier, len(rows) + len(cols))


def remote(src, dst, send, recv, **where):
    return pltpu.make_async_remote_copy(
        src_ref=src,
        dst_ref=dst,
        send_sem=send,
        recv_sem=recv,
        device_id=where,
        device_id_type=MESH,
    )


def chip_row(me, offset, core):
    y = (me // 8 + offset[0]) % 2
    z = ((me // 2) % 4 + offset[1]) % 4
    return y * 8 + z * 2 + core


def back_chip_row(me, offset, core):
    y = (me // 8 + offset[0]) % 2
    z = ((me // 2) % 4 + 4 - offset[1]) % 4
    return y * 8 + z * 2 + core


def hidden_kernel(feat, w, hid, fchunk, buf, hbuf, a_send, a_recv, g_send, g_recv, f_send, f_recv, lsem):
    me = lax.axis_index("row")
    core = me % 2
    other = 1 - core
    partner = me - core + other
    peers = [(me + k) % NROW for k in range(1, NROW)]
    greet(peers, [])

    def piece(r):
        return feat.at[:, pl.ds(pl.multiple_of(r * CHUNK, CHUNK), CHUNK)]

    swaps = []
    for k in range(1, NROW):
        r = peers[k - 1]
        copy = remote(piece(r), buf.at[me], a_send.at[k], a_recv.at[k], row=r)
        copy.start()
        swaps.append(copy)
    mine = pltpu.make_async_copy(piece(me), buf.at[me], lsem.at[0])
    mine.start()
    mine.wait()
    for copy in swaps:
        copy.wait_recv()
    chunk_t = buf[...].astype(f32).reshape(F, CHUNK).astype(bf16)
    fchunk[...] = chunk_t
    hbuf[...] = lax.dot_general(
        chunk_t, w[...], (((0,), (0,)), ((), ())), preferred_element_type=f32
    ).astype(bf16)

    slot = hid.at[me]
    sends = []
    for k, offset in enumerate(CHIPS):
        copy = remote(hbuf, slot, g_send.at[k], g_recv.at[k], row=chip_row(me, offset, core))
        copy.start()
        sends.append(copy)
    passes = [remote(hbuf, slot, f_send.at[7], f_recv.at[7], row=partner)]
    passes[0].start()
    keep = pltpu.make_async_copy(hbuf, slot, lsem.at[1])
    keep.start()
    for k, offset in enumerate(CHIPS):
        sends[k].wait_recv()
        got = hid.at[back_chip_row(me, offset, core)]
        copy = remote(got, got, f_send.at[k], f_recv.at[k], row=partner)
        copy.start()
        passes.append(copy)
    for copy in passes:
        copy.wait()
    for copy in sends + swaps:
        copy.wait_send()
    keep.wait()


def forward_kernel(rows, cols, count, tiles, hid, out, acc):
    step = pl.program_id(0)

    @pl.when(step == 0)
    def _():
        acc[...] = jnp.zeros_like(acc)

    n = count[0]
    for t in range(STEP):
        s = step * STEP + t
        r = jnp.where(s < n, rows[s], BR)
        acc[r] += jnp.dot(tiles[0, 0, t], hid[cols[s]], preferred_element_type=f32)

    @pl.when(step == pl.num_programs(0) - 1)
    def _():
        out[...] = acc[:BR].astype(bf16)


def backward_kernel(rows, cols, count, tiles, grad_t, out, acc):
    step = pl.program_id(0)

    @pl.when(step == 0)
    def _():
        acc[...] = jnp.zeros_like(acc)

    n = count[0]
    for t in range(STEP):
        s = step * STEP + t
        c = jnp.where(s < n, cols[s], BC)
        acc[c] += jnp.dot(grad_t[rows[s]], tiles[0, 0, t], preferred_element_type=f32)

    @pl.when(step == pl.num_programs(0) - 1)
    def _():
        out[...] = acc[:BC].astype(bf16)


def middle_kernel(part, cot, act, grad_t, rbuf, gbuf, r_send, r_recv, g_send, g_recv, lsem):
    me = lax.axis_index("col")
    peers = [(me + k) % NCOL for k in range(1, NCOL)]
    greet([], peers)
    adds = []
    for q in range(SUB):
        for k in range(1, NCOL):
            c = peers[k - 1]
            copy = remote(
                part.at[c, q], rbuf.at[q, me], r_send.at[q, k], r_recv.at[q, k], col=c
            )
            copy.start()
            adds.append(copy)
    own = []
    for q in range(SUB):
        copy = pltpu.make_async_copy(part.at[me, q], rbuf.at[q, me], lsem.at[q])
        copy.start()
        own.append(copy)
    gathers = []
    keeps = []
    for q in range(SUB):
        own[q].wait()
        for k in range(1, NCOL):
            adds[q * (NCOL - 1) + k - 1].wait_recv()
        pre = jnp.sum(rbuf[q].astype(f32), axis=0)
        sig = jax.nn.sigmoid(pre)
        span = pl.ds(q * BLK, BLK)
        act[span] = (pre * sig).astype(bf16)
        grad = cot[span].astype(f32) * sig * (1.0 + pre * (1.0 - sig))
        gbuf[q] = grad.T.astype(bf16)
        slot = grad_t.at[me, q]
        for k in range(1, NCOL):
            copy = remote(gbuf.at[q], slot, g_send.at[q, k], g_recv.at[q, k], col=peers[k - 1])
            copy.start()
            gathers.append(copy)
        keep = pltpu.make_async_copy(gbuf.at[q], slot, lsem.at[SUB + q])
        keep.start()
        keeps.append(keep)
    for copy in gathers:
        copy.wait()
    for copy in adds:
        copy.wait_send()
    for copy in keeps:
        copy.wait()


def last_kernel(
    back, w, fchunk, gw, gf, obuf, pbuf, sbuf, rbuf, gfbuf, gwbuf, gwrow, gwmine, gwcol,
    p_send, p_recv, r_send, r_recv, x_send, x_recv, w_send, w_recv, c_send, c_recv, lsem,
):
    me = lax.axis_index("row")
    col = lax.axis_index("col")
    core = me % 2
    other = 1 - core
    partner = me - core + other
    peers = [(me + k) % NROW for k in range(1, NROW)]
    cpeers = [(col + k) % NCOL for k in range(1, NCOL)]
    greet(peers, cpeers)
    order = [CHIPS[6], CHIPS[5], CHIPS[3], CHIPS[4], CHIPS[2], CHIPS[0], CHIPS[1], (0, 0)]
    pairs = []
    owns = []
    for k, offset in enumerate(order):
        copy = remote(
            back.at[chip_row(me, offset, other)], pbuf.at[k], p_send.at[k], p_recv.at[k], row=partner
        )
        copy.start()
        pairs.append(copy)
        own = pltpu.make_async_copy(back.at[chip_row(me, offset, core)], obuf.at[k], lsem.at[k])
        own.start()
        owns.append(own)
    sends = []
    for k, offset in enumerate(order[:7]):
        owns[k].wait()
        pairs[k].wait_recv()
        sbuf[k] = (obuf[k].astype(f32) + pbuf[k].astype(f32)).astype(bf16)
        copy = remote(
            sbuf.at[k], rbuf.at[k], r_send.at[k], r_recv.at[k], row=chip_row(me, offset, core)
        )
        copy.start()
        sends.append(copy)
    owns[7].wait()
    pairs[7].wait_recv()
    total = obuf[7].astype(f32) + pbuf[7].astype(f32)
    for k in range(7):
        sends[k].wait_recv()
        total = total + rbuf[k].astype(f32)
    hidden_grad = total.astype(bf16)
    weight = w[...]
    gw_part = jnp.zeros((F, F), f32)
    for q in range(SUB):
        block = hidden_grad[q]
        gf_t = jnp.dot(weight, block, preferred_element_type=f32)
        gfbuf[:, :, q * BLK : (q + 1) * BLK] = gf_t.reshape(NROW, PER, BLK).astype(bf16)
        gw_part = gw_part + lax.dot_general(
            fchunk[:, q * BLK : (q + 1) * BLK],
            block,
            (((1,), (1,)), ((), ())),
            preferred_element_type=f32,
        )
    gwbuf[...] = gw_part.reshape(NROW, PER, F)
    shares = []
    for k in range(1, NROW):
        r = peers[k - 1]
        copy = remote(gwbuf.at[r], gwrow.at[k], w_send.at[k], w_recv.at[k], row=r)
        copy.start()
        shares.append(copy)
    span = pl.ds(pl.multiple_of(me * CHUNK, CHUNK), CHUNK)
    swaps = []
    for k in range(1, NROW):
        r = peers[k - 1]
        copy = remote(gfbuf.at[r], gf.at[:, span], x_send.at[k], x_recv.at[k], row=r)
        copy.start()
        swaps.append(copy)
    keep = pltpu.make_async_copy(gfbuf.at[me], gf.at[:, span], lsem.at[8])
    keep.start()
    part = gwbuf[me]
    for k in range(1, NROW):
        shares[k - 1].wait_recv()
        part = part + gwrow[k]
    gwmine[...] = part
    spreads = []
    for k in range(1, NCOL):
        copy = remote(gwmine, gwcol.at[k], c_send.at[k], c_recv.at[k], col=cpeers[k - 1])
        copy.start()
        spreads.append(copy)
    for k in range(1, NCOL):
        spreads[k - 1].wait_recv()
        part = part + gwcol[k]
    gw[...] = part
    for copy in swaps:
        copy.wait()
    for copy in pairs + sends + shares + spreads:
        copy.wait_send()
    keep.wait()


def dma(*shape):
    return pltpu.SemaphoreType.DMA(shape)


def on_device(features, weight, tiles, tile_rows, tile_cols, tile_count, cotangent):
    sds = jax.ShapeDtypeStruct
    feat_t = features.T
    rows = tile_rows.reshape(TILE_CAP)
    cols = tile_cols.reshape(TILE_CAP)
    count = tile_count.reshape(1)

    hid, fchunk = pl.pallas_call(
        hidden_kernel,
        out_shape=(sds((NROW, CHUNK, F), bf16), sds((F, CHUNK), bf16)),
        in_specs=[any_spec(), vmem_spec()],
        out_specs=(any_spec(), vmem_spec()),
        scratch_shapes=[
            pltpu.VMEM((NROW, PER, CHUNK), bf16),
            pltpu.VMEM((CHUNK, F), bf16),
            dma(NROW), dma(NROW), dma(7), dma(7), dma(8), dma(8), dma(2),
        ],
        compiler_params=pltpu.CompilerParams(
            collective_id=0, has_side_effects=True, vmem_limit_bytes=16 * MIB
        ),
        name="hidden_gather",
    )(feat_t, weight)

    def tile_block(b, *_):
        return (0, 0, b, 0, 0)

    def whole(b, *_):
        return (0, 0, 0)

    def tile_call(kernel, name, blocks_in, blocks_out, panel):
        return pl.pallas_call(
            kernel,
            out_shape=sds((blocks_out, BLK, BLK), bf16),
            grid_spec=pltpu.PrefetchScalarGridSpec(
                num_scalar_prefetch=3,
                grid=(TILE_CAP // STEP,),
                in_specs=[
                    pl.BlockSpec((1, 1, STEP, BLK, BLK), tile_block),
                    pl.BlockSpec((blocks_in, BLK, BLK), whole),
                ],
                out_specs=pl.BlockSpec((blocks_out, BLK, BLK), whole),
                scratch_shapes=[pltpu.VMEM((blocks_out + 1, BLK, BLK), f32)],
            ),
            compiler_params=pltpu.CompilerParams(vmem_limit_bytes=24 * MIB),
            cost_estimate=pl.CostEstimate(
                flops=2 * TILE_CAP * BLK**3, bytes_accessed=11 * MIB, transcendentals=0
            ),
            name=name,
        )(rows, cols, count, tiles, panel)

    part = tile_call(forward_kernel, "forward_tiles", BC, BR, hid.reshape(BC, BLK, F))

    activated, grad_t = pl.pallas_call(
        middle_kernel,
        out_shape=(sds((CHUNK, F), bf16), sds((NCOL, SUB, F, BLK), bf16)),
        in_specs=[any_spec(), vmem_spec()],
        out_specs=(vmem_spec(), any_spec()),
        scratch_shapes=[
            pltpu.VMEM((SUB, NCOL, BLK, F), bf16),
            pltpu.VMEM((SUB, F, BLK), bf16),
            dma(SUB, NCOL), dma(SUB, NCOL), dma(SUB, NCOL), dma(SUB, NCOL), dma(2 * SUB),
        ],
        compiler_params=pltpu.CompilerParams(
            collective_id=1, has_side_effects=True, vmem_limit_bytes=16 * MIB
        ),
        name="activation",
    )(part.reshape(NCOL, SUB, BLK, F), cotangent)

    back = tile_call(backward_kernel, "backward_tiles", BR, BC, grad_t.reshape(BR, F, BLK))

    grad_weight, gf_t = pl.pallas_call(
        last_kernel,
        out_shape=(sds((PER, F), f32), sds((PER, NROW * CHUNK), bf16)),
        in_specs=[any_spec(), vmem_spec(), vmem_spec()],
        out_specs=(vmem_spec(), any_spec()),
        scratch_shapes=[
            pltpu.VMEM((8, SUB, F, BLK), bf16),
            pltpu.VMEM((8, SUB, F, BLK), bf16),
            pltpu.VMEM((7, SUB, F, BLK), bf16),
            pltpu.VMEM((7, SUB, F, BLK), bf16),
            pltpu.VMEM((NROW, PER, CHUNK), bf16),
            pltpu.VMEM((NROW, PER, F), f32),
            pltpu.VMEM((NROW, PER, F), f32),
            pltpu.VMEM((PER, F), f32),
            pltpu.VMEM((NCOL, PER, F), f32),
            dma(8), dma(8), dma(7), dma(7), dma(NROW), dma(NROW), dma(NROW), dma(NROW),
            dma(NCOL), dma(NCOL), dma(9),
        ],
        compiler_params=pltpu.CompilerParams(
            collective_id=2, has_side_effects=True, vmem_limit_bytes=16 * MIB
        ),
        name="gradients",
    )(back.reshape(NROW, SUB, F, BLK), weight, fchunk)
    return (activated, grad_weight, gf_t.T)


def solution(mesh):
    return jax.shard_map(
        on_device,
        mesh=mesh,
        in_specs=(
            P("col", "row"),
            P(),
            P("row", "col", None, None, None),
            P("row", "col", None),
            P("row", "col", None),
            P("row", "col"),
            P(("row", "col"), None),
        ),
        out_specs=(P(("row", "col"), None), P("row", None), P("col", "row")),
        check_vma=False,
    )
```

```python
import jax
import jax.numpy as jnp
from jax import lax
from jax.experimental import pallas as pl
from jax.experimental.pallas import tpu as pltpu
from jax.sharding import PartitionSpec as P

F = 128
BLK = 128
NROW = 16
NCOL = 8
BR = 32
BC = 64
TILE_CAP = 256
PANEL = BC * BLK
HALF = PANEL // 2
CHUNK = 512
SUB = CHUNK // BLK
PER = F // NROW
UNROLL = 32
MIB = 1024 * 1024
MESH = pl.DeviceIdType.MESH

f32 = jnp.float32
bf16 = jnp.bfloat16
i32 = jnp.int32

ORDER, TAKE, KEEP, LAST, HAS = range(5)


def any_spec():
    return pl.BlockSpec(memory_space=pl.ANY)


def vmem_spec():
    return pl.BlockSpec(memory_space=pltpu.VMEM)


def remote(src, dst, send, recv, **where):
    return pltpu.make_async_remote_copy(
        src_ref=src,
        dst_ref=dst,
        send_sem=send,
        recv_sem=recv,
        device_id=where,
        device_id_type=MESH,
    )


def make_plan(key_block, take, live, dead_block):
    n = TILE_CAP
    across = lax.broadcasted_iota(i32, (n, n), 1)
    down = lax.broadcasted_iota(i32, (n, n), 0)
    block = jnp.where(live, key_block, dead_block)
    block_r = jnp.broadcast_to(block, (n, n))
    block_c = block_r.T
    key_r = block_r * n + across
    key_c = block_c * n + down
    rank = jnp.sum(jnp.where(key_c < key_r, 1, 0), axis=0, keepdims=True)
    rank_c = jnp.broadcast_to(rank, (n, n)).T
    take_c = jnp.broadcast_to(take, (n, n)).T
    hit = rank_c == across
    order = jnp.sum(jnp.where(hit, down, 0), axis=0, keepdims=True)
    taken = jnp.sum(jnp.where(hit, take_c, 0), axis=0, keepdims=True)
    mine = jnp.sum(jnp.where(hit, block_c, 0), axis=0, keepdims=True)
    before = jnp.sum(jnp.where(rank_c == across - 1, block_c, 0), axis=0, keepdims=True)
    first = lax.broadcasted_iota(i32, (1, n), 1) == 0
    keep = jnp.where(first | (mine != before), 0, 1)
    last = jnp.maximum(jnp.sum(jnp.where(block_c <= across, 1, 0), axis=0, keepdims=True) - 1, 0)
    has = jnp.where(jnp.sum(jnp.where(block_c == across, 1, 0), axis=0, keepdims=True) > 0, 1, 0)
    return [order, taken, keep, last, has]


def layer_kernel(
    feat_in, weight, tiles, tile_rows, tile_cols, tile_count, cot,
    act, gw, gf,
    tv, feat, hid, prods, part, pbuf_col, gbuf, grad_t, back, pbuf, sbuf, rbuf,
    gfbuf, gwbuf, gwrow, gwmine, gwcol, plan_v, plan_s,
    l_sem, a_send, a_recv, f_send, f_recv, r_send, r_recv, g_send, g_recv,
    p_send, p_recv, s_send, s_recv, x_send, x_recv, w_send, w_recv, c_send, c_recv,
):
    me = lax.axis_index("row")
    col = lax.axis_index("col")
    yh = me // 8
    z = (me // 2) % 4
    core = me % 2
    other = 1 - core

    def at(dy, dz, k):
        return ((yh + dy) % 2) * 8 + ((z + dz) % 4) * 2 + k

    partner = at(0, 0, other)
    up, down, across = at(0, 1, core), at(0, 3, core), at(1, 0, core)
    peers = [(me + k) % NROW for k in range(1, NROW)]
    cpeers = [(col + k) % NCOL for k in range(1, NCOL)]

    tile_copy = pltpu.make_async_copy(tiles.at[0, 0], tv, l_sem.at[0])
    tile_copy.start()
    own_copy = pltpu.make_async_copy(feat_in, feat.at[me], l_sem.at[1])
    own_copy.start()

    barrier = pltpu.get_barrier_semaphore()
    for r in peers:
        pl.semaphore_signal(barrier, inc=1, device_id={"row": r}, device_id_type=MESH)
    for c in cpeers:
        pl.semaphore_signal(barrier, inc=1, device_id={"col": c}, device_id_type=MESH)
    pl.semaphore_wait(barrier, len(peers) + len(cpeers))

    started = []

    def half(ref, h):
        return ref.at[:, pl.ds(h * HALF, HALF)]

    def send(src, slab, h, index, to):
        dst = feat.at[slab] if h is None else half(feat.at[slab], h)
        copy = remote(src, dst, a_send.at[index], a_recv.at[index], row=to)
        copy.start()
        started.append(copy)
        return copy

    def pass_on(slab, h, index, to):
        return send(half(feat.at[slab], h), slab, h, index, to)

    got = {}
    got["d", 0] = send(half(feat_in, 0), me, 0, 0, up)
    got["u", 1] = send(half(feat_in, 1), me, 1, 3, down)
    got["y", 0] = send(half(feat_in, 0), me, 0, 4, across)
    got["y", 1] = send(half(feat_in, 1), me, 1, 5, across)
    got["d", 1] = send(half(feat_in, 1), me, 1, 1, up)
    got["u", 0] = send(half(feat_in, 0), me, 0, 2, down)
    got["c", 2] = send(feat_in, me, None, 6, partner)

    live = lax.broadcasted_iota(i32, (1, TILE_CAP), 1) < tile_count[0, 0]
    forward = make_plan(tile_rows[0], tile_cols[0], live, BR)
    backward = make_plan(tile_cols[0], tile_rows[0], live, BC)
    for i, line in enumerate(forward + backward):
        plan_v[i : i + 1, :] = line
    plan_copy = pltpu.make_async_copy(plan_v, plan_s, l_sem.at[2])
    plan_copy.start()

    handed = []

    def hand(slab, h):
        index = len(handed)
        piece = half(feat.at[slab], h)
        copy = remote(piece, piece, f_send.at[index], f_recv.at[index], row=partner)
        copy.start()
        handed.append(copy)

    below, above = at(0, 3, core), at(0, 1, core)
    far = at(0, 2, core)
    y_own, y_below, y_above, y_far = (at(1, d, core) for d in (0, 3, 1, 2))

    got["d", 0].wait_recv()
    got["far", 0] = pass_on(below, 0, 7, up)
    hand(below, 0)
    got["u", 1].wait_recv()
    got["far", 1] = pass_on(above, 1, 8, down)
    hand(above, 1)
    got["y", 0].wait_recv()
    got["yd", 0] = pass_on(y_own, 0, 9, up)
    got["y", 1].wait_recv()
    got["yu", 1] = pass_on(y_own, 1, 12, down)
    got["yd", 1] = pass_on(y_own, 1, 10, up)
    got["yu", 0] = pass_on(y_own, 0, 11, down)
    hand(y_own, 0)
    hand(y_own, 1)
    got["d", 1].wait_recv()
    hand(below, 1)
    got["u", 0].wait_recv()
    hand(above, 0)
    got["far", 0].wait_recv()
    hand(far, 0)
    got["far", 1].wait_recv()
    hand(far, 1)
    got["yd", 0].wait_recv()
    got["yfar", 0] = pass_on(y_below, 0, 13, up)
    got["yu", 1].wait_recv()
    got["yfar", 1] = pass_on(y_above, 1, 14, down)
    hand(y_below, 0)
    hand(y_above, 1)
    got["yd", 1].wait_recv()
    hand(y_below, 1)
    got["yu", 0].wait_recv()
    hand(y_above, 0)
    got["yfar", 0].wait_recv()
    hand(y_far, 0)
    got["yfar", 1].wait_recv()
    hand(y_far, 1)
    got["c", 2].wait_recv()
    own_copy.wait()
    for copy in handed:
        copy.wait_recv()

    def columns(start, width):
        span = pl.ds(pl.multiple_of(start, BLK), width)
        return feat[:, :, span].astype(f32).reshape(F, width).astype(bf16)

    w = weight[...]

    def hidden_step(i, carry):
        for t in range(8):
            b = i * 8 + t
            hid[b] = lax.dot_general(
                columns(b * BLK, BLK), w, (((0,), (0,)), ((), ())), preferred_element_type=f32
            ).astype(bf16)
        return carry

    lax.fori_loop(0, BC // 8, hidden_step, 0)

    plan_copy.wait()
    tile_copy.wait()

    def forward_step(i, total):
        for t in range(UNROLL):
            p = i * UNROLL + t
            keep = plan_s[KEEP, p].astype(f32)
            total = total * keep + jnp.dot(
                tv[plan_s[ORDER, p]], hid[plan_s[TAKE, p]], preferred_element_type=f32
            )
            prods[p] = total.astype(bf16)
        return total

    lax.fori_loop(0, TILE_CAP // UNROLL, forward_step, jnp.zeros((BLK, F), f32))
    for b in range(BR):
        has = plan_s[HAS, b].astype(f32)
        part[b // SUB, b % SUB] = (prods[plan_s[LAST, b]].astype(f32) * has).astype(bf16)

    adds = []
    for q in range(SUB):
        for k in range(1, NCOL):
            c = cpeers[k - 1]
            copy = remote(
                part.at[c, q], pbuf_col.at[q, k], r_send.at[q, k], r_recv.at[q, k], col=c
            )
            copy.start()
            adds.append(copy)
    gathers = []
    for q in range(SUB):
        pre = part[col, q].astype(f32)
        for k in range(1, NCOL):
            adds[q * (NCOL - 1) + k - 1].wait_recv()
            pre = pre + pbuf_col[q, k].astype(f32)
        sig = jax.nn.sigmoid(pre)
        span = pl.ds(q * BLK, BLK)
        act[span] = (pre * sig).astype(bf16)
        grad = cot[span].astype(f32) * sig * (1.0 + pre * (1.0 - sig))
        grad_block = grad.T.astype(bf16)
        gbuf[q] = grad_block
        grad_t[col * SUB + q] = grad_block
        slot = grad_t.at[col * SUB + q]
        for k in range(1, NCOL):
            copy = remote(gbuf.at[q], slot, g_send.at[q, k], g_recv.at[q, k], col=cpeers[k - 1])
            copy.start()
            gathers.append(copy)
    for copy in gathers:
        copy.wait_recv()

    def backward_step(i, total):
        for t in range(UNROLL):
            p = i * UNROLL + t
            keep = plan_s[5 + KEEP, p].astype(f32)
            total = total * keep + jnp.dot(
                grad_t[plan_s[5 + TAKE, p]], tv[plan_s[5 + ORDER, p]], preferred_element_type=f32
            )
            prods[p] = total.astype(bf16)
        return total

    lax.fori_loop(0, TILE_CAP // UNROLL, backward_step, jnp.zeros((F, BLK), f32))
    for b in range(BC):
        has = plan_s[5 + HAS, b].astype(f32)
        back[b // SUB, b % SUB] = (prods[plan_s[5 + LAST, b]].astype(f32) * has).astype(bf16)

    order = [(1, 2), (0, 2), (1, 1), (1, 3), (1, 0), (0, 1), (0, 3), (0, 0)]
    pairs = []
    for k, (dy, dz) in enumerate(order):
        copy = remote(
            back.at[at(dy, dz, other)], pbuf.at[k], p_send.at[k], p_recv.at[k], row=partner
        )
        copy.start()
        pairs.append(copy)
    sums = []
    for k, (dy, dz) in enumerate(order[:7]):
        pairs[k].wait_recv()
        sbuf[k] = (back[at(dy, dz, core)].astype(f32) + pbuf[k].astype(f32)).astype(bf16)
        copy = remote(sbuf.at[k], rbuf.at[k], s_send.at[k], s_recv.at[k], row=at(dy, dz, core))
        copy.start()
        sums.append(copy)
    feat_chunk = columns(me * CHUNK, CHUNK)
    pairs[7].wait_recv()
    for copy in sums:
        copy.wait_recv()
    gw_part = jnp.zeros((F, F), f32)
    for q in range(SUB):
        total = back[me, q].astype(f32) + pbuf[7, q].astype(f32)
        for k in range(7):
            total = total + rbuf[k, q].astype(f32)
        block = total.astype(bf16)
        gf_t = jnp.dot(w, block, preferred_element_type=f32)
        gfbuf[:, :, q * BLK : (q + 1) * BLK] = gf_t.reshape(NROW, PER, BLK).astype(bf16)
        gw_part = gw_part + lax.dot_general(
            feat_chunk[:, q * BLK : (q + 1) * BLK],
            block,
            (((1,), (1,)), ((), ())),
            preferred_element_type=f32,
        )
    gwbuf[...] = gw_part.reshape(NROW, PER, F)

    shares = []
    for k in range(1, NROW):
        r = peers[k - 1]
        copy = remote(gwbuf.at[r], gwrow.at[k], w_send.at[k], w_recv.at[k], row=r)
        copy.start()
        shares.append(copy)
    place = pl.ds(pl.multiple_of(me * CHUNK, CHUNK), CHUNK)
    swaps = []
    for k in range(1, NROW):
        r = peers[k - 1]
        copy = remote(gfbuf.at[r], gf.at[:, place], x_send.at[k], x_recv.at[k], row=r)
        copy.start()
        swaps.append(copy)
    gf[:, place] = gfbuf[me]
    gw_sum = gwbuf[me]
    for k in range(1, NROW):
        shares[k - 1].wait_recv()
        gw_sum = gw_sum + gwrow[k]
    gwmine[...] = gw_sum
    spreads = []
    for k in range(1, NCOL):
        copy = remote(gwmine, gwcol.at[k], c_send.at[k], c_recv.at[k], col=cpeers[k - 1])
        copy.start()
        spreads.append(copy)
    for k in range(1, NCOL):
        spreads[k - 1].wait_recv()
        gw_sum = gw_sum + gwcol[k]
    gw[...] = gw_sum
    for copy in swaps:
        copy.wait()
    for copy in started + handed + adds + gathers + pairs + sums + shares + spreads:
        copy.wait_send()


def dma(*shape):
    return pltpu.SemaphoreType.DMA(shape)


def on_device(features, weight, tiles, tile_rows, tile_cols, tile_count, cotangent):
    sds = jax.ShapeDtypeStruct
    activated, grad_weight, gf_t = pl.pallas_call(
        layer_kernel,
        out_shape=(sds((CHUNK, F), bf16), sds((PER, F), f32), sds((PER, PANEL), bf16)),
        in_specs=[
            any_spec(), vmem_spec(), any_spec(), vmem_spec(), vmem_spec(), vmem_spec(), vmem_spec(),
        ],
        out_specs=(vmem_spec(), vmem_spec(), vmem_spec()),
        scratch_shapes=[
            pltpu.VMEM((TILE_CAP, BLK, BLK), bf16),
            pltpu.VMEM((NROW, PER, PANEL), bf16),
            pltpu.VMEM((BC, BLK, F), bf16),
            pltpu.VMEM((TILE_CAP, BLK, BLK), bf16),
            pltpu.VMEM((NCOL, SUB, BLK, F), bf16),
            pltpu.VMEM((SUB, NCOL, BLK, F), bf16),
            pltpu.VMEM((SUB, F, BLK), bf16),
            pltpu.VMEM((BR, F, BLK), bf16),
            pltpu.VMEM((NROW, SUB, F, BLK), bf16),
            pltpu.VMEM((8, SUB, F, BLK), bf16),
            pltpu.VMEM((7, SUB, F, BLK), bf16),
            pltpu.VMEM((7, SUB, F, BLK), bf16),
            pltpu.VMEM((NROW, PER, CHUNK), bf16),
            pltpu.VMEM((NROW, PER, F), f32),
            pltpu.VMEM((NROW, PER, F), f32),
            pltpu.VMEM((PER, F), f32),
            pltpu.VMEM((NCOL, PER, F), f32),
            pltpu.VMEM((16, TILE_CAP), i32),
            pltpu.SMEM((16, TILE_CAP), i32),
            dma(3), dma(15), dma(15), dma(14), dma(14),
            dma(SUB, NCOL), dma(SUB, NCOL), dma(SUB, NCOL), dma(SUB, NCOL),
            dma(8), dma(8), dma(7), dma(7), dma(NROW), dma(NROW), dma(NROW), dma(NROW),
            dma(NCOL), dma(NCOL),
        ],
        compiler_params=pltpu.CompilerParams(
            collective_id=0, has_side_effects=True, vmem_limit_bytes=48 * MIB
        ),
        cost_estimate=pl.CostEstimate(
            flops=4 * TILE_CAP * BLK**3, bytes_accessed=11 * MIB, transcendentals=CHUNK * F
        ),
        name="graph_layer",
    )(features.T, weight, tiles, tile_rows[0], tile_cols[0], tile_count, cotangent)
    return (activated, grad_weight, gf_t.T)


def solution(mesh):
    return jax.shard_map(
        on_device,
        mesh=mesh,
        in_specs=(
            P("col", "row"),
            P(),
            P("row", "col", None, None, None),
            P("row", "col", None),
            P("row", "col", None),
            P("row", "col"),
            P(("row", "col"), None),
        ),
        out_specs=(P(("row", "col"), None), P("row", None), P("col", "row")),
        check_vma=False,
    )
```

```python
import jax
import jax.numpy as jnp
from jax import lax
from jax.experimental import pallas as pl
from jax.experimental.pallas import tpu as pltpu
from jax.sharding import PartitionSpec as P

F = 128
BLK = 128
NROW = 16
NCOL = 8
BR = 32
BC = 64
TILE_CAP = 256
PANEL = BC * BLK
HALF = PANEL // 2
CHUNK = 512
SUB = CHUNK // BLK
PER = F // NROW
UNROLL = 32
MIB = 1024 * 1024
MESH = pl.DeviceIdType.MESH

f32 = jnp.float32
bf16 = jnp.bfloat16
i32 = jnp.int32

ORDER, TAKE, KEEP, LAST, HAS = range(5)


def any_spec():
    return pl.BlockSpec(memory_space=pl.ANY)


def vmem_spec():
    return pl.BlockSpec(memory_space=pltpu.VMEM)


def start_remote(pending, src, dst, send, recv, **where):
    copy = pltpu.make_async_remote_copy(
        src_ref=src,
        dst_ref=dst,
        send_sem=send,
        recv_sem=recv,
        device_id=where,
        device_id_type=MESH,
    )
    copy.start()
    pending.append(copy)
    return copy


def make_plan(key_block, take, live, dead_block):
    n = TILE_CAP
    across = lax.broadcasted_iota(i32, (n, n), 1)
    down = lax.broadcasted_iota(i32, (n, n), 0)
    block = jnp.where(live, key_block, dead_block)
    block_r = jnp.broadcast_to(block, (n, n))
    block_c = block_r.T
    key_r = block_r * n + across
    key_c = block_c * n + down
    rank = jnp.sum(jnp.where(key_c < key_r, 1, 0), axis=0, keepdims=True)
    rank_c = jnp.broadcast_to(rank, (n, n)).T
    take_c = jnp.broadcast_to(take, (n, n)).T
    hit = rank_c == across
    order = jnp.sum(jnp.where(hit, down, 0), axis=0, keepdims=True)
    taken = jnp.sum(jnp.where(hit, take_c, 0), axis=0, keepdims=True)
    mine = jnp.sum(jnp.where(hit, block_c, 0), axis=0, keepdims=True)
    before = jnp.sum(jnp.where(rank_c == across - 1, block_c, 0), axis=0, keepdims=True)
    first = lax.broadcasted_iota(i32, (1, n), 1) == 0
    keep = jnp.where(first | (mine != before), 0, 1)
    last = jnp.maximum(jnp.sum(jnp.where(block_c <= across, 1, 0), axis=0, keepdims=True) - 1, 0)
    has = jnp.where(jnp.sum(jnp.where(block_c == across, 1, 0), axis=0, keepdims=True) > 0, 1, 0)
    return [order, taken, keep, last, has]


def layer_kernel(
    feat_in, weight_in, tiles, rows_in, cols_in, count_in, cot_in,
    act, gw, gf,
    weight, rows_v, cols_v, count_v, cot,
    tv, feat, hid, prods, part, x_far, x_sum, x_below, x_above, y_sum, y_got, mine, grad_t,
    back, slabs, pbuf, sbuf, rbuf, gwbuf, gwpair, gwsum, gwrow, gwmine, gwcol, plan_v, plan_s,
    l_sem, a_send, a_recv, f_send, f_recv, r_send, r_recv, g_send, g_recv,
    p_send, p_recv, s_send, s_recv, w_send, w_recv, c_send, c_recv,
):
    me = lax.axis_index("row")
    col = lax.axis_index("col")
    yh = me // 8
    z = (me // 2) % 4
    core = me % 2
    other = 1 - core

    def at(dy, dz, k):
        return ((yh + dy) % 2) * 8 + ((z + dz) % 4) * 2 + k

    partner = at(0, 0, other)
    up, down, across = at(0, 1, core), at(0, 3, core), at(1, 0, core)
    peers = [partner] + [at(dy, dz, core) for dy in (0, 1) for dz in range(4) if dy + dz]
    cpeers = [(col + k) % NCOL for k in range(1, NCOL)]

    tile_copy = pltpu.make_async_copy(tiles.at[0, 0], tv, l_sem.at[0])
    tile_copy.start()
    own_copy = pltpu.make_async_copy(feat_in, feat.at[me], l_sem.at[1])
    own_copy.start()
    small = []
    for i, (src, dst) in enumerate(
        [(rows_in, rows_v), (cols_in, cols_v), (count_in, count_v), (weight_in, weight), (cot_in, cot)]
    ):
        copy = pltpu.make_async_copy(src, dst, l_sem.at[3 + i])
        copy.start()
        small.append(copy)

    barrier = pltpu.get_barrier_semaphore()
    for r in peers:
        pl.semaphore_signal(barrier, inc=1, device_id={"row": r}, device_id_type=MESH)
    for c in cpeers:
        pl.semaphore_signal(barrier, inc=1, device_id={"col": c}, device_id_type=MESH)
    pl.semaphore_wait(barrier, len(peers) + len(cpeers))

    pending = []

    def half(ref, h):
        return ref.at[:, pl.ds(h * HALF, HALF)]

    def send(src, slab, h, index, to):
        dst = feat.at[slab] if h is None else half(feat.at[slab], h)
        copy = start_remote(pending, src, dst, a_send.at[index], a_recv.at[index], row=to)
        return copy

    def pass_on(slab, h, index, to):
        return send(half(feat.at[slab], h), slab, h, index, to)

    got = {}
    got["d", 0] = send(half(feat_in, 0), me, 0, 0, up)
    got["u", 1] = send(half(feat_in, 1), me, 1, 3, down)
    got["y", 0] = send(half(feat_in, 0), me, 0, 4, across)
    got["y", 1] = send(half(feat_in, 1), me, 1, 5, across)
    got["d", 1] = send(half(feat_in, 1), me, 1, 1, up)
    got["u", 0] = send(half(feat_in, 0), me, 0, 2, down)
    got["c", 2] = send(feat_in, me, None, 6, partner)

    for copy in small:
        copy.wait()
    live = lax.broadcasted_iota(i32, (1, TILE_CAP), 1) < count_v[0, 0]
    forward = make_plan(rows_v[...], cols_v[...], live, BR)
    backward = make_plan(cols_v[...], rows_v[...], live, BC)
    for i, line in enumerate(forward + backward):
        plan_v[i : i + 1, :] = line
    plan_copy = pltpu.make_async_copy(plan_v, plan_s, l_sem.at[2])
    plan_copy.start()

    handed = []

    def hand(slab, h):
        index = len(handed)
        piece = half(feat.at[slab], h)
        copy = start_remote(pending, piece, piece, f_send.at[index], f_recv.at[index], row=partner)
        handed.append(copy)

    below, above = at(0, 3, core), at(0, 1, core)
    far = at(0, 2, core)
    y_own, y_below, y_above, y_far = (at(1, d, core) for d in (0, 3, 1, 2))

    got["d", 0].wait_recv()
    got["far", 0] = pass_on(below, 0, 7, up)
    hand(below, 0)
    got["u", 1].wait_recv()
    got["far", 1] = pass_on(above, 1, 8, down)
    hand(above, 1)
    got["y", 0].wait_recv()
    got["yd", 0] = pass_on(y_own, 0, 9, up)
    got["y", 1].wait_recv()
    got["yu", 1] = pass_on(y_own, 1, 12, down)
    got["yd", 1] = pass_on(y_own, 1, 10, up)
    got["yu", 0] = pass_on(y_own, 0, 11, down)
    hand(y_own, 0)
    hand(y_own, 1)
    got["d", 1].wait_recv()
    hand(below, 1)
    got["u", 0].wait_recv()
    hand(above, 0)
    got["far", 0].wait_recv()
    got["yfar", 0] = pass_on(far, 0, 13, across)
    hand(far, 0)
    got["far", 1].wait_recv()
    got["yfar", 1] = pass_on(far, 1, 14, across)
    hand(far, 1)
    got["yd", 0].wait_recv()
    hand(y_below, 0)
    got["yu", 1].wait_recv()
    hand(y_above, 1)
    got["yd", 1].wait_recv()
    hand(y_below, 1)
    got["yu", 0].wait_recv()
    hand(y_above, 0)
    got["yfar", 0].wait_recv()
    hand(y_far, 0)
    got["yfar", 1].wait_recv()
    hand(y_far, 1)
    got["c", 2].wait_recv()
    own_copy.wait()
    for copy in handed:
        copy.wait_recv()

    def columns(start, width):
        span = pl.ds(pl.multiple_of(start, BLK), width)
        return feat[:, :, span].astype(f32).reshape(F, width).astype(bf16)

    w = weight[...]

    def hidden_step(i, carry):
        for t in range(8):
            b = i * 8 + t
            hid[b] = lax.dot_general(
                columns(b * BLK, BLK), w, (((0,), (0,)), ((), ())), preferred_element_type=f32
            ).astype(bf16)
        return carry

    lax.fori_loop(0, BC // 8, hidden_step, 0)

    plan_copy.wait()
    tile_copy.wait()

    def forward_step(i, total):
        for t in range(UNROLL):
            p = i * UNROLL + t
            keep = plan_s[KEEP, p].astype(f32)
            total = total * keep + jnp.dot(
                tv[plan_s[ORDER, p]], hid[plan_s[TAKE, p]], preferred_element_type=f32
            )
            prods[p] = total.astype(bf16)
        return total

    lax.fori_loop(0, TILE_CAP // UNROLL, forward_step, jnp.zeros((BLK, F), f32))
    for b in range(BR):
        has = plan_s[HAS, b].astype(f32)
        part[b % SUB, b // SUB] = (prods[plan_s[LAST, b]].astype(f32) * has).astype(bf16)

    x = col // 2
    yl = col % 2

    def spot(dx, dy):
        return ((x + dx) % 4) * 2 + (yl + dy) % 2

    c_up, c_down, c_across = spot(1, 0), spot(3, 0), spot(0, 1)

    def both(q, dx):
        return part.at[q, pl.ds(((x + dx) % 4) * 2, 2)]

    def add_up(src, dst, q, index):
        return start_remote(
            pending, src, dst.at[q], r_send.at[index, q], r_recv.at[index, q], col=c_up
        )

    def add_down(src, dst, q, index):
        return start_remote(
            pending, src, dst.at[q], r_send.at[index, q], r_recv.at[index, q], col=c_down
        )

    far_in = {}
    from_below = {}
    from_above = {}
    far_in[0] = add_up(both(0, 2), x_far, 0, 0)
    far_in[2] = add_down(both(2, 2), x_far, 2, 0)
    far_in[1] = add_up(both(1, 2), x_far, 1, 0)
    far_in[3] = add_down(both(3, 2), x_far, 3, 0)
    from_below[2] = add_up(both(2, 1), x_below, 2, 1)
    from_above[0] = add_down(both(0, 3), x_above, 0, 2)

    def joined(q, dx):
        far_in[q].wait_recv()
        x_sum[q] = (both(q, dx)[...].astype(f32) + x_far[q].astype(f32)).astype(bf16)
        return x_sum.at[q]

    from_below[0] = add_up(joined(0, 1), x_below, 0, 1)
    from_above[2] = add_down(joined(2, 3), x_above, 2, 2)
    from_below[3] = add_up(both(3, 1), x_below, 3, 1)
    from_above[1] = add_down(both(1, 3), x_above, 1, 2)
    from_below[1] = add_up(joined(1, 1), x_below, 1, 1)
    from_above[3] = add_down(joined(3, 3), x_above, 3, 2)

    y_in = {}
    gathers = {}

    def gather(dx, dy, q, way):
        to, rx, ry = {
            "up": (c_up, (dx + 3) % 4, dy),
            "down": (c_down, (dx + 1) % 4, dy),
            "across": (c_across, dx, 1 - dy),
        }[way]
        piece = grad_t.at[spot(dx, dy) * SUB + q]
        index = rx * 2 + ry
        gathers[rx, ry, q] = start_remote(
            pending, piece, piece, g_send.at[index, q], g_recv.at[index, q], col=to
        )

    def here(dx, dy, q):
        gathers.pop((dx, dy, q)).wait_recv()

    def across_sum(q):
        from_below[q].wait_recv()
        from_above[q].wait_recv()

        def side(dy):
            y = (yl + dy) % 2
            return (
                part[q, spot(0, dy)].astype(f32)
                + x_below[q, y].astype(f32)
                + x_above[q, y].astype(f32)
            )

        y_sum[q] = side(1).astype(bf16)
        y_in[q] = start_remote(
            pending, y_sum.at[q], y_got.at[q], r_send.at[3, q], r_recv.at[3, q], col=c_across
        )
        mine[q] = side(0)

    def activate(q):
        y_in[q].wait_recv()
        pre = mine[q] + y_got[q].astype(f32)
        sig = jax.nn.sigmoid(pre)
        span = pl.ds(q * BLK, BLK)
        act[span] = (pre * sig).astype(bf16)
        grad = cot[span].astype(f32) * sig * (1.0 + pre * (1.0 - sig))
        grad_t[col * SUB + q] = grad.T.astype(bf16)
        for way in ("across", "up", "down") if q % 2 == 0 else ("up", "down", "across"):
            gather(0, 0, q, way)

    across_sum(0)
    across_sum(2)
    activate(0)
    activate(2)
    across_sum(1)
    across_sum(3)
    here(0, 1, 0)
    gather(0, 1, 0, "up")
    gather(0, 1, 0, "down")
    here(0, 1, 2)
    gather(0, 1, 2, "down")
    gather(0, 1, 2, "up")
    activate(1)
    activate(3)
    here(3, 0, 0)
    gather(3, 0, 0, "up")
    here(1, 0, 2)
    gather(1, 0, 2, "down")
    here(3, 1, 0)
    gather(3, 1, 0, "up")
    here(1, 1, 2)
    gather(1, 1, 2, "down")
    here(3, 0, 1)
    gather(3, 0, 1, "up")
    gather(3, 0, 1, "across")
    here(1, 0, 3)
    gather(1, 0, 3, "down")
    gather(1, 0, 3, "across")
    here(3, 0, 3)
    gather(3, 0, 3, "across")
    here(1, 0, 1)
    gather(1, 0, 1, "across")
    here(2, 0, 1)
    gather(2, 0, 1, "across")
    here(2, 0, 3)
    gather(2, 0, 3, "across")
    for key in list(gathers):
        here(*key)

    def backward_step(i, total):
        for t in range(UNROLL):
            p = i * UNROLL + t
            keep = plan_s[5 + KEEP, p].astype(f32)
            total = total * keep + jnp.dot(
                grad_t[plan_s[5 + TAKE, p]], tv[plan_s[5 + ORDER, p]], preferred_element_type=f32
            )
            prods[p] = total.astype(bf16)
        return total

    lax.fori_loop(0, TILE_CAP // UNROLL, backward_step, jnp.zeros((F, BLK), f32))

    chips = [(0, 1), (0, 2), (0, 3), (1, 0), (1, 1), (1, 2), (1, 3), (0, 0)]
    pairs = {}

    def panel_step(i, carry):
        for t in range(8):
            b = i * 8 + t
            has = plan_s[5 + HAS, b].astype(f32)
            block = (prods[plan_s[5 + LAST, b]].astype(f32) * has).astype(bf16)
            back[b] = block
            out = jnp.dot(w, block, preferred_element_type=f32)
            span = pl.ds(pl.multiple_of(b * BLK, BLK), BLK)
            slabs[:, :, span] = out.reshape(NROW, PER, BLK).astype(bf16)
        return carry

    def start_pairs(h, items):
        for dy, dz in items:
            k = chips.index((dy, dz))
            pairs[dy, dz, h] = start_remote(
                pending,
                half(slabs.at[at(dy, dz, other)], h),
                pbuf.at[h, k],
                p_send.at[h, k],
                p_recv.at[h, k],
                row=partner,
            )

    lax.fori_loop(0, BC // 16, panel_step, 0)
    start_pairs(0, [(0, 2), (1, 2), (0, 1), (1, 1), (0, 3), (1, 3), (1, 0), (0, 0)])
    lax.fori_loop(BC // 16, BC // 8, panel_step, 0)
    start_pairs(1, [(1, 2), (1, 1), (1, 3), (1, 0), (0, 2), (0, 1), (0, 3), (0, 0)])

    def pair_sum(dy, dz, h):
        pairs[dy, dz, h].wait_recv()
        k = chips.index((dy, dz))
        own = slabs[at(dy, dz, core), :, h * HALF : (h + 1) * HALF]
        return own.astype(f32) + pbuf[h, k].astype(f32)

    def pass_sum(value, h, k, to):
        sbuf[h, k] = value.astype(bf16)
        return start_remote(
            pending, sbuf.at[h, k], rbuf.at[h, k], s_send.at[h, k], s_recv.at[h, k], row=to
        )

    sums = {}
    for dz in (2, 1, 3):
        for dy in (1, 0):
            k = chips.index((dy, dz))
            sums[dy, dz, 0] = pass_sum(pair_sum(dy, dz, 0), 0, k, at(0, dz, core))
    for dz in (2, 1, 3, 0):
        k = chips.index((1, dz))
        sums[1, dz, 1] = pass_sum(pair_sum(1, dz, 1), 1, k, across)

    def weight_step(i, total):
        for t in range(8):
            b = i * 8 + t
            total = total + lax.dot_general(
                columns(b * BLK, BLK), back[b], (((1,), (1,)), ((), ())), preferred_element_type=f32
            )
        return total

    gw_part = lax.fori_loop(0, BC // 8, weight_step, jnp.zeros((F, F), f32))
    for r in range(NROW):
        gwbuf[r % 2, r // 2] = gw_part[r * PER : (r + 1) * PER]
    gw_pair = start_remote(
        pending, gwbuf.at[other], gwpair, w_send.at[7], w_recv.at[7], row=partner
    )

    for dz in (2, 1, 3):
        k = chips.index((0, dz))
        value = pair_sum(0, dz, 1)
        sums[1, dz, 1].wait_recv()
        value = value + rbuf[1, chips.index((1, dz))].astype(f32)
        sums[0, dz, 1] = pass_sum(value, 1, k, at(0, dz, core))

    value = pair_sum(1, 0, 0)
    for dz in (1, 2, 3):
        sums[1, dz, 0].wait_recv()
        value = value + rbuf[0, chips.index((1, dz))].astype(f32)
    sums[1, 0, 0] = pass_sum(value, 0, chips.index((1, 0)), across)

    gw_pair.wait_recv()
    gwsum[...] = gwbuf[core] + gwpair[...]
    shares = []
    for k, (dy, dz) in enumerate(chips[:7]):
        chip = ((yh + dy) % 2) * 4 + (z + dz) % 4
        shares.append(
            start_remote(
                pending,
                gwsum.at[chip],
                gwrow.at[k],
                w_send.at[k],
                w_recv.at[k],
                row=at(dy, dz, core),
            )
        )

    total = pair_sum(0, 0, 1)
    sums[1, 0, 1].wait_recv()
    total = total + rbuf[1, chips.index((1, 0))].astype(f32)
    for dz in (1, 2, 3):
        sums[0, dz, 1].wait_recv()
        total = total + rbuf[1, chips.index((0, dz))].astype(f32)
    gf[:, HALF:] = total.astype(bf16)

    gw_sum = gwsum[me // 2]
    for k in range(7):
        shares[k].wait_recv()
        gw_sum = gw_sum + gwrow[k]
    gwmine[...] = gw_sum
    spreads = []
    for k in range(1, NCOL):
        spreads.append(
            start_remote(
                pending, gwmine, gwcol.at[k], c_send.at[k], c_recv.at[k], col=cpeers[k - 1]
            )
        )

    total = pair_sum(0, 0, 0)
    for dy, dz in ((0, 1), (0, 2), (0, 3), (1, 0)):
        sums[dy, dz, 0].wait_recv()
        total = total + rbuf[0, chips.index((dy, dz))].astype(f32)
    gf[:, :HALF] = total.astype(bf16)

    for k in range(1, NCOL):
        spreads[k - 1].wait_recv()
        gw_sum = gw_sum + gwcol[k]
    gw[...] = gw_sum
    for copy in pending:
        copy.wait_send()


def dma(*shape):
    return pltpu.SemaphoreType.DMA(shape)


def on_device(features, weight, tiles, tile_rows, tile_cols, tile_count, cotangent):
    sds = jax.ShapeDtypeStruct
    activated, grad_weight, gf_t = pl.pallas_call(
        layer_kernel,
        out_shape=(sds((CHUNK, F), bf16), sds((PER, F), f32), sds((PER, PANEL), bf16)),
        in_specs=[any_spec()] * 7,
        out_specs=(vmem_spec(), vmem_spec(), vmem_spec()),
        scratch_shapes=[
            pltpu.VMEM((F, F), bf16),
            pltpu.VMEM((1, TILE_CAP), i32),
            pltpu.VMEM((1, TILE_CAP), i32),
            pltpu.VMEM((1, 1), i32),
            pltpu.VMEM((CHUNK, F), bf16),
            pltpu.VMEM((TILE_CAP, BLK, BLK), bf16),
            pltpu.VMEM((NROW, PER, PANEL), bf16),
            pltpu.VMEM((BC, BLK, F), bf16),
            pltpu.VMEM((TILE_CAP, BLK, BLK), bf16),
            pltpu.VMEM((SUB, NCOL, BLK, F), bf16),
            pltpu.VMEM((SUB, 2, BLK, F), bf16),
            pltpu.VMEM((SUB, 2, BLK, F), bf16),
            pltpu.VMEM((SUB, 2, BLK, F), bf16),
            pltpu.VMEM((SUB, 2, BLK, F), bf16),
            pltpu.VMEM((SUB, BLK, F), bf16),
            pltpu.VMEM((SUB, BLK, F), bf16),
            pltpu.VMEM((SUB, BLK, F), f32),
            pltpu.VMEM((BR, F, BLK), bf16),
            pltpu.VMEM((BC, F, BLK), bf16),
            pltpu.VMEM((NROW, PER, PANEL), bf16),
            pltpu.VMEM((2, 8, PER, HALF), bf16),
            pltpu.VMEM((2, 7, PER, HALF), bf16),
            pltpu.VMEM((2, 7, PER, HALF), bf16),
            pltpu.VMEM((2, 8, PER, F), f32),
            pltpu.VMEM((8, PER, F), f32),
            pltpu.VMEM((8, PER, F), f32),
            pltpu.VMEM((7, PER, F), f32),
            pltpu.VMEM((PER, F), f32),
            pltpu.VMEM((NCOL, PER, F), f32),
            pltpu.VMEM((16, TILE_CAP), i32),
            pltpu.SMEM((16, TILE_CAP), i32),
            dma(8), dma(15), dma(15), dma(14), dma(14),
            dma(4, SUB), dma(4, SUB), dma(NCOL, SUB), dma(NCOL, SUB),
            dma(2, 8), dma(2, 8), dma(2, 7), dma(2, 7), dma(8), dma(8),
            dma(NCOL), dma(NCOL),
        ],
        compiler_params=pltpu.CompilerParams(
            collective_id=0, has_side_effects=True, vmem_limit_bytes=60 * MIB
        ),
        cost_estimate=pl.CostEstimate(
            flops=4 * TILE_CAP * BLK**3, bytes_accessed=11 * MIB, transcendentals=CHUNK * F
        ),
        name="graph_layer",
    )(features.T, weight, tiles, tile_rows[0], tile_cols[0], tile_count, cotangent)
    return (activated, grad_weight, gf_t.T)


def solution(mesh):
    return jax.shard_map(
        on_device,
        mesh=mesh,
        in_specs=(
            P("col", "row"),
            P(),
            P("row", "col", None, None, None),
            P("row", "col", None),
            P("row", "col", None),
            P("row", "col"),
            P(("row", "col"), None),
        ),
        out_specs=(P(("row", "col"), None), P("row", None), P("col", "row")),
        check_vma=False,
    )
```

```python
import jax
import jax.numpy as jnp
from jax import lax
from jax.experimental import pallas as pl
from jax.experimental.pallas import tpu as pltpu
from jax.sharding import PartitionSpec as P

F = 128
BLK = 128
NROW = 16
NCOL = 8
BR = 32
BC = 64
TILE_CAP = 256
PANEL = BC * BLK
HALF = PANEL // 2
CHUNK = 512
SUB = CHUNK // BLK
PER = F // NROW
UNROLL = 32
MIB = 1024 * 1024
MESH = pl.DeviceIdType.MESH

f32 = jnp.float32
bf16 = jnp.bfloat16
i32 = jnp.int32

NSUB = 4
WIDE = SUB // NSUB
SUM_PATH = ("yx", "xy", "yx", "xy")
GATHER_PATH = ("xy", "yx", "xy", "yx")
SCHEDULE = "f0 f1 f2 f3 s0 s1 s2 s3 e0 e1 e2 e3 g0 g1 g2 g3"

ORDER, TAKE, KEEP, LAST, HAS = range(5)


def any_spec():
    return pl.BlockSpec(memory_space=pl.ANY)


def vmem_spec():
    return pl.BlockSpec(memory_space=pltpu.VMEM)


def start_remote(pending, src, dst, send, recv, **where):
    copy = pltpu.make_async_remote_copy(
        src_ref=src,
        dst_ref=dst,
        send_sem=send,
        recv_sem=recv,
        device_id=where,
        device_id_type=MESH,
    )
    copy.start()
    pending.append(copy)
    return copy


def make_plan(key_block, take, live, dead_block):
    n = TILE_CAP
    across = lax.broadcasted_iota(i32, (n, n), 1)
    down = lax.broadcasted_iota(i32, (n, n), 0)
    block = jnp.where(live, key_block, dead_block)
    block_r = jnp.broadcast_to(block, (n, n))
    block_c = block_r.T
    key_r = block_r * n + across
    key_c = block_c * n + down
    rank = jnp.sum(jnp.where(key_c < key_r, 1, 0), axis=0, keepdims=True)
    rank_c = jnp.broadcast_to(rank, (n, n)).T
    take_c = jnp.broadcast_to(take, (n, n)).T
    hit = rank_c == across
    order = jnp.sum(jnp.where(hit, down, 0), axis=0, keepdims=True)
    taken = jnp.sum(jnp.where(hit, take_c, 0), axis=0, keepdims=True)
    mine = jnp.sum(jnp.where(hit, block_c, 0), axis=0, keepdims=True)
    before = jnp.sum(jnp.where(rank_c == across - 1, block_c, 0), axis=0, keepdims=True)
    first = lax.broadcasted_iota(i32, (1, n), 1) == 0
    keep = jnp.where(first | (mine != before), 0, 1)
    last = jnp.maximum(jnp.sum(jnp.where(block_c <= across, 1, 0), axis=0, keepdims=True) - 1, 0)
    has = jnp.where(jnp.sum(jnp.where(block_c == across, 1, 0), axis=0, keepdims=True) > 0, 1, 0)
    return [order, taken, keep, last, has]


def layer_kernel(
    feat_in, weight_in, tiles, rows_in, cols_in, count_in, cot_in,
    act, gw, gf,
    weight, rows_v, cols_v, count_v, cot,
    tv, feat, hid, prods, part, x_sum, x_in, y_in, d_in, grad_t,
    back, slabs, pbuf, sbuf, rbuf, gwbuf, gwpair, gwsum, gwrow, gwmine, gwcol, plan_v, plan_s,
    l_sem, a_send, a_recv, f_send, f_recv, r_send, r_recv, g_send, g_recv,
    p_send, p_recv, s_send, s_recv, w_send, w_recv, c_send, c_recv,
):
    me = lax.axis_index("row")
    col = lax.axis_index("col")
    yh = me // 8
    z = (me // 2) % 4
    core = me % 2
    other = 1 - core

    def at(dy, dz, k):
        return ((yh + dy) % 2) * 8 + ((z + dz) % 4) * 2 + k

    partner = at(0, 0, other)
    up, down, across = at(0, 1, core), at(0, 3, core), at(1, 0, core)
    peers = [partner] + [at(dy, dz, core) for dy in (0, 1) for dz in range(4) if dy + dz]
    cpeers = [(col + k) % NCOL for k in range(1, NCOL)]

    tile_copy = pltpu.make_async_copy(tiles.at[0, 0], tv, l_sem.at[0])
    tile_copy.start()
    own_copy = pltpu.make_async_copy(feat_in, feat.at[me], l_sem.at[1])
    own_copy.start()
    small = []
    for i, (src, dst) in enumerate(
        [(rows_in, rows_v), (cols_in, cols_v), (count_in, count_v), (weight_in, weight), (cot_in, cot)]
    ):
        copy = pltpu.make_async_copy(src, dst, l_sem.at[3 + i])
        copy.start()
        small.append(copy)

    barrier = pltpu.get_barrier_semaphore()
    for r in peers:
        pl.semaphore_signal(barrier, inc=1, device_id={"row": r}, device_id_type=MESH)
    for c in cpeers:
        pl.semaphore_signal(barrier, inc=1, device_id={"col": c}, device_id_type=MESH)
    pl.semaphore_wait(barrier, len(peers) + len(cpeers))

    pending = []

    def half(ref, h):
        return ref.at[:, pl.ds(h * HALF, HALF)]

    def send(src, slab, h, index, to):
        dst = feat.at[slab] if h is None else half(feat.at[slab], h)
        copy = start_remote(pending, src, dst, a_send.at[index], a_recv.at[index], row=to)
        return copy

    def pass_on(slab, h, index, to):
        return send(half(feat.at[slab], h), slab, h, index, to)

    got = {}
    got["d", 0] = send(half(feat_in, 0), me, 0, 0, up)
    got["u", 1] = send(half(feat_in, 1), me, 1, 3, down)
    got["y", 0] = send(half(feat_in, 0), me, 0, 4, across)
    got["y", 1] = send(half(feat_in, 1), me, 1, 5, across)
    got["d", 1] = send(half(feat_in, 1), me, 1, 1, up)
    got["u", 0] = send(half(feat_in, 0), me, 0, 2, down)
    got["c", 2] = send(feat_in, me, None, 6, partner)

    for copy in small:
        copy.wait()
    live = lax.broadcasted_iota(i32, (1, TILE_CAP), 1) < count_v[0, 0]
    forward = make_plan(rows_v[...], cols_v[...], live, BR)
    backward = make_plan(cols_v[...], rows_v[...], live, BC)
    for i, line in enumerate(forward + backward):
        plan_v[i : i + 1, :] = line
    plan_copy = pltpu.make_async_copy(plan_v, plan_s, l_sem.at[2])
    plan_copy.start()

    handed = []

    def hand(slab, h):
        index = len(handed)
        piece = half(feat.at[slab], h)
        copy = start_remote(pending, piece, piece, f_send.at[index], f_recv.at[index], row=partner)
        handed.append(copy)

    below, above = at(0, 3, core), at(0, 1, core)
    far = at(0, 2, core)
    y_own, y_below, y_above, y_far = (at(1, d, core) for d in (0, 3, 1, 2))

    got["d", 0].wait_recv()
    got["far", 0] = pass_on(below, 0, 7, up)
    hand(below, 0)
    got["u", 1].wait_recv()
    got["far", 1] = pass_on(above, 1, 8, down)
    hand(above, 1)
    got["y", 0].wait_recv()
    got["yd", 0] = pass_on(y_own, 0, 9, up)
    got["y", 1].wait_recv()
    got["yu", 1] = pass_on(y_own, 1, 12, down)
    got["yd", 1] = pass_on(y_own, 1, 10, up)
    got["yu", 0] = pass_on(y_own, 0, 11, down)
    hand(y_own, 0)
    hand(y_own, 1)
    got["d", 1].wait_recv()
    hand(below, 1)
    got["u", 0].wait_recv()
    hand(above, 0)
    got["far", 0].wait_recv()
    got["yfar", 0] = pass_on(far, 0, 13, across)
    hand(far, 0)
    got["far", 1].wait_recv()
    got["yfar", 1] = pass_on(far, 1, 14, across)
    hand(far, 1)
    got["yd", 0].wait_recv()
    hand(y_below, 0)
    got["yu", 1].wait_recv()
    hand(y_above, 1)
    got["yd", 1].wait_recv()
    hand(y_below, 1)
    got["yu", 0].wait_recv()
    hand(y_above, 0)
    got["yfar", 0].wait_recv()
    hand(y_far, 0)
    got["yfar", 1].wait_recv()
    hand(y_far, 1)
    got["c", 2].wait_recv()
    own_copy.wait()
    for copy in handed:
        copy.wait_recv()

    def columns(start, width):
        span = pl.ds(pl.multiple_of(start, BLK), width)
        return feat[:, :, span].astype(f32).reshape(F, width).astype(bf16)

    w = weight[...]

    def hidden_step(i, carry):
        for t in range(8):
            b = i * 8 + t
            hid[b] = lax.dot_general(
                columns(b * BLK, BLK), w, (((0,), (0,)), ((), ())), preferred_element_type=f32
            ).astype(bf16)
        return carry

    lax.fori_loop(0, BC // 8, hidden_step, 0)

    plan_copy.wait()
    tile_copy.wait()

    def forward_step(i, total):
        for t in range(UNROLL):
            p = i * UNROLL + t
            keep = plan_s[KEEP, p].astype(f32)
            total = total * keep + jnp.dot(
                tv[plan_s[ORDER, p]], hid[plan_s[TAKE, p]], preferred_element_type=f32
            )
            prods[p] = total.astype(bf16)
        return total

    lax.fori_loop(0, TILE_CAP // UNROLL, forward_step, jnp.zeros((BLK, F), f32))
    for b in range(BR):
        has = plan_s[HAS, b].astype(f32)
        sub, place = b % SUB // WIDE, b % SUB % WIDE * BLK
        block = (prods[plan_s[LAST, b]].astype(f32) * has).astype(bf16)
        part[sub, b // SUB, place : place + BLK] = block

    x = col // 2
    yl = col % 2

    def spot(dx, dy):
        return ((x + dx) % 4) * 2 + (yl + dy) % 2

    def both(q, dx):
        return part.at[q, pl.ds(((x + dx) % 4) * 2, 2)]

    def add_to(src, dst, q, index, to):
        return start_remote(
            pending, src, dst, r_send.at[index, q], r_recv.at[index, q], col=to
        )

    x_got = {}
    y_got = {}
    every = [(2, 1), (2, 0), (1, 1), (3, 1), (1, 0), (3, 0), (0, 1)]
    def first(q):
        if SUM_PATH[q] == "yx":
            for dx in (2, 1, 3, 0):
                src = part.at[q, spot(dx, 1)]
                y_got[q, dx] = add_to(src, y_in.at[q, dx], q, 4 + dx, spot(0, 1))
        elif SUM_PATH[q] == "xy":
            for dx in (2, 1, 3):
                x_got[q, dx] = add_to(both(q, dx), x_in.at[q, dx], q, dx, spot(dx, 0))
        else:
            for k, (dx, dy) in enumerate(every):
                src = part.at[q, spot(dx, dy)]
                x_got[q, k] = add_to(src, d_in.at[q, k], q, 8 + k, spot(dx, dy))

    def second(q):
        if SUM_PATH[q] == "yx":
            for dx in (2, 1, 3):
                y_got[q, dx].wait_recv()
                x_sum[q, dx] = (
                    part[q, spot(dx, 0)].astype(f32) + y_in[q, dx].astype(f32)
                ).astype(bf16)
                x_got[q, dx] = add_to(x_sum.at[q, dx], x_in.at[q, dx, 0], q, dx, spot(dx, 0))
        elif SUM_PATH[q] == "xy":
            side = part[q, spot(0, 1)].astype(f32)
            for dx in (2, 1, 3):
                x_got[q, dx].wait_recv()
                side = side + x_in[q, dx, (yl + 1) % 2].astype(f32)
            x_sum[q, 0] = side.astype(bf16)
            y_got[q, 0] = add_to(x_sum.at[q, 0], y_in.at[q, 0], q, 4, spot(0, 1))

    def summed(q):
        pre = part[q, col].astype(f32)
        if SUM_PATH[q] == "direct":
            for k in range(NCOL - 1):
                x_got[q, k].wait_recv()
                pre = pre + d_in[q, k].astype(f32)
            return pre
        for dx in (2, 1, 3):
            if SUM_PATH[q] == "yx":
                x_got[q, dx].wait_recv()
                pre = pre + x_in[q, dx, 0].astype(f32)
            else:
                pre = pre + x_in[q, dx, yl].astype(f32)
        y_got[q, 0].wait_recv()
        return pre + y_in[q, 0].astype(f32)

    gathers = {}

    def gather(dx, dy, q, tx, ty):
        piece = grad_t.at[pl.ds(spot(dx, dy) * SUB + q * WIDE, WIDE)]
        rx, ry = (dx - tx) % 4, (dy - ty) % 2
        index = rx * 2 + ry
        gathers[rx, ry, q] = start_remote(
            pending, piece, piece, g_send.at[index, q], g_recv.at[index, q], col=spot(tx, ty)
        )

    def here(dx, dy, q):
        gathers.pop((dx, dy, q)).wait_recv()

    def finish(q):
        pre = summed(q)
        sig = jax.nn.sigmoid(pre)
        span = pl.ds(q * WIDE * BLK, WIDE * BLK)
        grad = cot[span].astype(f32) * sig * (1.0 + pre * (1.0 - sig))
        for i in range(WIDE):
            block = grad[i * BLK : (i + 1) * BLK].T
            grad_t[col * SUB + q * WIDE + i] = block.astype(bf16)
        if GATHER_PATH[q] == "yx":
            ways = [(0, 1), (2, 0), (1, 0), (3, 0)]
        elif GATHER_PATH[q] == "xy":
            ways = [(2, 0), (1, 0), (3, 0), (0, 1)]
        else:
            ways = every
        for tx, ty in ways:
            gather(0, 0, q, tx, ty)
        act[span] = (pre * sig).astype(bf16)

    def spread(q):
        if GATHER_PATH[q] == "yx":
            here(0, 1, q)
            for tx in (2, 1, 3):
                gather(0, 1, q, tx, 0)
        elif GATHER_PATH[q] == "xy":
            for dx in (3, 1, 2):
                here(dx, 0, q)
                gather(dx, 0, q, 0, 1)

    def drain(q):
        got = [v for d in (x_got, y_got) for key, v in d.items() if key[0] == q]
        for copy in got:
            copy.wait_send()
            pending[:] = [other_copy for other_copy in pending if other_copy is not copy]

    steps = {"f": first, "s": second, "e": finish, "g": spread, "d": drain}
    for step in SCHEDULE.split():
        steps[step[0]](int(step[1]))
    for key in list(gathers):
        here(*key)

    def backward_step(i, total):
        for t in range(UNROLL):
            p = i * UNROLL + t
            keep = plan_s[5 + KEEP, p].astype(f32)
            total = total * keep + jnp.dot(
                grad_t[plan_s[5 + TAKE, p]], tv[plan_s[5 + ORDER, p]], preferred_element_type=f32
            )
            prods[p] = total.astype(bf16)
        return total

    lax.fori_loop(0, TILE_CAP // UNROLL, backward_step, jnp.zeros((F, BLK), f32))

    chips = [(0, 1), (0, 2), (0, 3), (1, 0), (1, 1), (1, 2), (1, 3), (0, 0)]
    pairs = {}

    def panel_step(i, carry):
        for t in range(8):
            b = i * 8 + t
            has = plan_s[5 + HAS, b].astype(f32)
            block = (prods[plan_s[5 + LAST, b]].astype(f32) * has).astype(bf16)
            back[b] = block
            out = jnp.dot(w, block, preferred_element_type=f32)
            span = pl.ds(pl.multiple_of(b * BLK, BLK), BLK)
            slabs[:, :, span] = out.reshape(NROW, PER, BLK).astype(bf16)
        return carry

    def start_pairs(h, items):
        for dy, dz in items:
            k = chips.index((dy, dz))
            pairs[dy, dz, h] = start_remote(
                pending,
                half(slabs.at[at(dy, dz, other)], h),
                pbuf.at[h, k],
                p_send.at[h, k],
                p_recv.at[h, k],
                row=partner,
            )

    lax.fori_loop(0, BC // 16, panel_step, 0)
    start_pairs(0, [(0, 2), (1, 2), (0, 1), (1, 1), (0, 3), (1, 3), (1, 0), (0, 0)])
    lax.fori_loop(BC // 16, BC // 8, panel_step, 0)
    start_pairs(1, [(1, 2), (1, 1), (1, 3), (1, 0), (0, 2), (0, 1), (0, 3), (0, 0)])

    def pair_sum(dy, dz, h):
        pairs[dy, dz, h].wait_recv()
        k = chips.index((dy, dz))
        own = slabs[at(dy, dz, core), :, h * HALF : (h + 1) * HALF]
        return own.astype(f32) + pbuf[h, k].astype(f32)

    def pass_sum(value, h, k, to):
        sbuf[h, k] = value.astype(bf16)
        return start_remote(
            pending, sbuf.at[h, k], rbuf.at[h, k], s_send.at[h, k], s_recv.at[h, k], row=to
        )

    sums = {}
    for dz in (2, 1, 3):
        for dy in (1, 0):
            k = chips.index((dy, dz))
            sums[dy, dz, 0] = pass_sum(pair_sum(dy, dz, 0), 0, k, at(0, dz, core))
    for dz in (2, 1, 3, 0):
        k = chips.index((1, dz))
        sums[1, dz, 1] = pass_sum(pair_sum(1, dz, 1), 1, k, across)

    def weight_step(i, total):
        for t in range(8):
            b = i * 8 + t
            total = total + lax.dot_general(
                columns(b * BLK, BLK), back[b], (((1,), (1,)), ((), ())), preferred_element_type=f32
            )
        return total

    gw_part = lax.fori_loop(0, BC // 8, weight_step, jnp.zeros((F, F), f32))
    for r in range(NROW):
        gwbuf[r % 2, r // 2] = gw_part[r * PER : (r + 1) * PER]
    gw_pair = start_remote(
        pending, gwbuf.at[other], gwpair, w_send.at[7], w_recv.at[7], row=partner
    )

    for dz in (2, 1, 3):
        k = chips.index((0, dz))
        value = pair_sum(0, dz, 1)
        sums[1, dz, 1].wait_recv()
        value = value + rbuf[1, chips.index((1, dz))].astype(f32)
        sums[0, dz, 1] = pass_sum(value, 1, k, at(0, dz, core))

    value = pair_sum(1, 0, 0)
    for dz in (1, 2, 3):
        sums[1, dz, 0].wait_recv()
        value = value + rbuf[0, chips.index((1, dz))].astype(f32)
    sums[1, 0, 0] = pass_sum(value, 0, chips.index((1, 0)), across)

    gw_pair.wait_recv()
    gwsum[...] = gwbuf[core] + gwpair[...]
    shares = []
    for k, (dy, dz) in enumerate(chips[:7]):
        chip = ((yh + dy) % 2) * 4 + (z + dz) % 4
        shares.append(
            start_remote(
                pending,
                gwsum.at[chip],
                gwrow.at[k],
                w_send.at[k],
                w_recv.at[k],
                row=at(dy, dz, core),
            )
        )

    total = pair_sum(0, 0, 1)
    sums[1, 0, 1].wait_recv()
    total = total + rbuf[1, chips.index((1, 0))].astype(f32)
    for dz in (1, 2, 3):
        sums[0, dz, 1].wait_recv()
        total = total + rbuf[1, chips.index((0, dz))].astype(f32)
    gf[:, HALF:] = total.astype(bf16)

    gw_sum = gwsum[me // 2]
    for k in range(7):
        shares[k].wait_recv()
        gw_sum = gw_sum + gwrow[k]
    gwmine[...] = gw_sum
    spreads = []
    for k in range(1, NCOL):
        spreads.append(
            start_remote(
                pending, gwmine, gwcol.at[k], c_send.at[k], c_recv.at[k], col=cpeers[k - 1]
            )
        )

    total = pair_sum(0, 0, 0)
    for dy, dz in ((0, 1), (0, 2), (0, 3), (1, 0)):
        sums[dy, dz, 0].wait_recv()
        total = total + rbuf[0, chips.index((dy, dz))].astype(f32)
    gf[:, :HALF] = total.astype(bf16)

    for k in range(1, NCOL):
        spreads[k - 1].wait_recv()
        gw_sum = gw_sum + gwcol[k]
    gw[...] = gw_sum
    for copy in pending:
        copy.wait_send()


def write_kernel(act, gw, gf, act_out, gw_out, gf_out, act_v, gw_v, gf_v, sem):
    def copies(ends, base):
        return [
            pltpu.make_async_copy(src, dst, sem.at[base + i]) for i, (src, dst) in enumerate(ends)
        ]

    reads = copies([(gf, gf_v), (act, act_v), (gw, gw_v)], 0)
    writes = copies([(gf_v, gf_out), (act_v, act_out), (gw_v, gw_out)], 3)
    for copy in reads:
        copy.start()
    for read, write in zip(reads, writes):
        read.wait()
        write.start()
    for copy in writes:
        copy.wait()


def dma(*shape):
    return pltpu.SemaphoreType.DMA(shape)


def on_device(features, weight, tiles, tile_rows, tile_cols, tile_count, cotangent):
    sds = jax.ShapeDtypeStruct
    shapes = (sds((CHUNK, F), bf16), sds((PER, F), f32), sds((PER, PANEL), bf16))
    outs = pl.pallas_call(
        layer_kernel,
        out_shape=shapes,
        in_specs=[any_spec()] * 7,
        out_specs=(vmem_spec(), vmem_spec(), vmem_spec()),
        scratch_shapes=[
            pltpu.VMEM((F, F), bf16),
            pltpu.VMEM((1, TILE_CAP), i32),
            pltpu.VMEM((1, TILE_CAP), i32),
            pltpu.VMEM((1, 1), i32),
            pltpu.VMEM((CHUNK, F), bf16),
            pltpu.VMEM((TILE_CAP, BLK, BLK), bf16),
            pltpu.VMEM((NROW, PER, PANEL), bf16),
            pltpu.VMEM((BC, BLK, F), bf16),
            pltpu.VMEM((TILE_CAP, BLK, BLK), bf16),
            pltpu.VMEM((NSUB, NCOL, WIDE * BLK, F), bf16),
            pltpu.VMEM((NSUB, 4, WIDE * BLK, F), bf16),
            pltpu.VMEM((NSUB, 4, 2, WIDE * BLK, F), bf16),
            pltpu.VMEM((NSUB, 4, WIDE * BLK, F), bf16),
            pltpu.VMEM((NSUB, NCOL - 1, WIDE * BLK, F), bf16),
            pltpu.VMEM((BR, F, BLK), bf16),
            pltpu.VMEM((BC, F, BLK), bf16),
            pltpu.VMEM((NROW, PER, PANEL), bf16),
            pltpu.VMEM((2, 8, PER, HALF), bf16),
            pltpu.VMEM((2, 7, PER, HALF), bf16),
            pltpu.VMEM((2, 7, PER, HALF), bf16),
            pltpu.VMEM((2, 8, PER, F), f32),
            pltpu.VMEM((8, PER, F), f32),
            pltpu.VMEM((8, PER, F), f32),
            pltpu.VMEM((7, PER, F), f32),
            pltpu.VMEM((PER, F), f32),
            pltpu.VMEM((NCOL, PER, F), f32),
            pltpu.VMEM((16, TILE_CAP), i32),
            pltpu.SMEM((16, TILE_CAP), i32),
            dma(8), dma(15), dma(15), dma(14), dma(14),
            dma(16, NSUB), dma(16, NSUB), dma(NCOL, NSUB), dma(NCOL, NSUB),
            dma(2, 8), dma(2, 8), dma(2, 7), dma(2, 7), dma(8), dma(8),
            dma(NCOL), dma(NCOL),
        ],
        compiler_params=pltpu.CompilerParams(
            collective_id=0, has_side_effects=True, vmem_limit_bytes=60 * MIB
        ),
        cost_estimate=pl.CostEstimate(
            flops=4 * TILE_CAP * BLK**3, bytes_accessed=11 * MIB, transcendentals=CHUNK * F
        ),
        name="graph_layer",
    )(features.T, weight, tiles, tile_rows[0], tile_cols[0], tile_count, cotangent)
    activated, grad_weight, gf_t = pl.pallas_call(
        write_kernel,
        out_shape=shapes,
        in_specs=[any_spec()] * 3,
        out_specs=(any_spec(),) * 3,
        scratch_shapes=[pltpu.VMEM(x.shape, x.dtype) for x in shapes] + [dma(6)],
        compiler_params=pltpu.CompilerParams(vmem_limit_bytes=60 * MIB),
        name="write_results",
    )(*outs)
    return (activated, grad_weight, gf_t.T)


def solution(mesh):
    return jax.shard_map(
        on_device,
        mesh=mesh,
        in_specs=(
            P("col", "row"),
            P(),
            P("row", "col", None, None, None),
            P("row", "col", None),
            P("row", "col", None),
            P("row", "col"),
            P(("row", "col"), None),
        ),
        out_specs=(P(("row", "col"), None), P("row", None), P("col", "row")),
        check_vma=False,
    )
```

```python
import jax
import jax.numpy as jnp
from jax import lax
from jax.experimental import pallas as pl
from jax.experimental.pallas import tpu as pltpu
from jax.sharding import PartitionSpec as P

F = 128
BLK = 128
NROW = 16
NCOL = 8
BR = 32
BC = 64
TILE_CAP = 256
PANEL = BC * BLK
HALF = PANEL // 2
CHUNK = 512
SUB = CHUNK // BLK
PER = F // NROW
UNROLL = 64
MIB = 1024 * 1024
MESH = pl.DeviceIdType.MESH

f32 = jnp.float32
bf16 = jnp.bfloat16
i32 = jnp.int32

NSUB = 4
WIDE = SUB // NSUB
SUM_PATH = ("yx", "xy", "yx", "xy")
GATHER_PATH = ("xy", "yx", "xy", "yx")
SCHEDULE = "f0 f1 f2 f3 s0 s1 s2 s3 e0 e1 e2 e3 g0 g1 g2 g3"

ORDER, TAKE, KEEP, LAST, HAS = range(5)


def any_spec():
    return pl.BlockSpec(memory_space=pl.ANY)


def vmem_spec():
    return pl.BlockSpec(memory_space=pltpu.VMEM)


def start_remote(pending, src, dst, send, recv, **where):
    copy = pltpu.make_async_remote_copy(
        src_ref=src,
        dst_ref=dst,
        send_sem=send,
        recv_sem=recv,
        device_id=where,
        device_id_type=MESH,
    )
    copy.start()
    pending.append(copy)
    return copy


def make_plan(key_block, take, live, dead_block):
    n = TILE_CAP
    across = lax.broadcasted_iota(i32, (n, n), 1)
    down = lax.broadcasted_iota(i32, (n, n), 0)
    block = jnp.where(live, key_block, dead_block)
    block_r = jnp.broadcast_to(block, (n, n))
    block_c = block_r.T
    key_r = block_r * n + across
    key_c = block_c * n + down
    rank = jnp.sum(jnp.where(key_c < key_r, 1, 0), axis=0, keepdims=True)
    rank_c = jnp.broadcast_to(rank, (n, n)).T
    take_c = jnp.broadcast_to(take, (n, n)).T
    hit = rank_c == across
    order = jnp.sum(jnp.where(hit, down, 0), axis=0, keepdims=True)
    taken = jnp.sum(jnp.where(hit, take_c, 0), axis=0, keepdims=True)
    mine = jnp.sum(jnp.where(hit, block_c, 0), axis=0, keepdims=True)
    before = jnp.sum(jnp.where(rank_c == across - 1, block_c, 0), axis=0, keepdims=True)
    first = lax.broadcasted_iota(i32, (1, n), 1) == 0
    keep = jnp.where(first | (mine != before), 0, 1)
    last = jnp.maximum(jnp.sum(jnp.where(block_c <= across, 1, 0), axis=0, keepdims=True) - 1, 0)
    has = jnp.where(jnp.sum(jnp.where(block_c == across, 1, 0), axis=0, keepdims=True) > 0, 1, 0)
    return [order, taken, keep, last, has]


def layer_kernel(
    feat_in, weight_in, tiles, rows_in, cols_in, count_in, cot_in,
    act, gw, gf,
    weight, rows_v, cols_v, count_v, cot,
    tv, feat, feat_n, hid, prods, part, x_sum, x_in, y_in, d_in, grad_t,
    back, slabs, pbuf, sbuf, rbuf, gwbuf, gwpair, gwsum, gwrow, gwmine, gwcol, plan_v, plan_s,
    l_sem, a_send, a_recv, f_send, f_recv, r_send, r_recv, g_send, g_recv,
    p_send, p_recv, s_send, s_recv, w_send, w_recv, c_send, c_recv,
):
    me = lax.axis_index("row")
    col = lax.axis_index("col")
    yh = me // 8
    z = (me // 2) % 4
    core = me % 2
    other = 1 - core

    def at(dy, dz, k):
        return ((yh + dy) % 2) * 8 + ((z + dz) % 4) * 2 + k

    partner = at(0, 0, other)
    across = at(1, 0, core)
    peers = [partner] + [at(dy, dz, core) for dy in (0, 1) for dz in range(4) if dy + dz]
    cpeers = [(col + k) % NCOL for k in range(1, NCOL)]

    tile_copy = pltpu.make_async_copy(tiles.at[0, 0], tv, l_sem.at[0])
    tile_copy.start()
    own_copy = pltpu.make_async_copy(feat_in, feat.at[me], l_sem.at[1])
    own_copy.start()
    small = []
    for i, (src, dst) in enumerate(
        [(rows_in, rows_v), (cols_in, cols_v), (count_in, count_v), (weight_in, weight), (cot_in, cot)]
    ):
        copy = pltpu.make_async_copy(src, dst, l_sem.at[3 + i])
        copy.start()
        small.append(copy)

    barrier = pltpu.get_barrier_semaphore()
    for r in peers:
        pl.semaphore_signal(barrier, inc=1, device_id={"row": r}, device_id_type=MESH)
    for c in cpeers:
        pl.semaphore_signal(barrier, inc=1, device_id={"col": c}, device_id_type=MESH)
    pl.semaphore_wait(barrier, len(peers) + len(cpeers))

    pending = []

    def half(ref, h):
        return ref.at[:, pl.ds(h * HALF, HALF)]

    got = {}

    def send(dy, dz, h, ty, tz):
        piece = half(feat.at[at(dy, dz, core)], h)
        src = half(feat_in, h) if (dy, dz) == (0, 0) else piece
        ry, rz = (dy - ty) % 2, (dz - tz) % 4
        index = h * 8 + ry * 4 + rz
        got[ry, rz, h] = start_remote(
            pending, src, piece, a_send.at[index], a_recv.at[index], row=at(ty, tz, core)
        )

    send(0, 0, 1, 1, 0)
    for tz in (2, 1, 3):
        send(0, 0, 0, 0, tz)
    send(0, 0, 0, 1, 0)
    for tz in (2, 1, 3):
        send(0, 0, 1, 0, tz)
    own_hand = start_remote(
        pending, feat_in, feat.at[me], f_send.at[0], f_recv.at[0], row=partner
    )

    for copy in small:
        copy.wait()
    live = lax.broadcasted_iota(i32, (1, TILE_CAP), 1) < count_v[0, 0]
    forward = make_plan(rows_v[...], cols_v[...], live, BR)
    backward = make_plan(cols_v[...], rows_v[...], live, BC)
    for i, line in enumerate(forward + backward):
        plan_v[i : i + 1, :] = line
    plan_copy = pltpu.make_async_copy(plan_v, plan_s, l_sem.at[2])
    plan_copy.start()

    handed = [own_hand]

    def hand(dy, dz, h):
        index = len(handed)
        piece = half(feat.at[at(dy, dz, core)], h)
        handed.append(
            start_remote(
                pending, piece, piece, f_send.at[index], f_recv.at[index], row=partner
            )
        )

    got[1, 0, 1].wait_recv()
    for tz in (2, 1, 3):
        send(1, 0, 1, 0, tz)
    hand(1, 0, 1)
    for dz in (1, 3, 2):
        got[0, dz, 0].wait_recv()
        send(0, dz, 0, 1, 0)
        hand(0, dz, 0)
    for dy, dz, h in (
        (1, 0, 0), (0, 1, 1), (0, 3, 1), (0, 2, 1), (1, 1, 0), (1, 3, 0), (1, 2, 0),
        (1, 1, 1), (1, 3, 1), (1, 2, 1),
    ):
        got[dy, dz, h].wait_recv()
        hand(dy, dz, h)
    own_copy.wait()
    for copy in handed:
        copy.wait_recv()

    w = weight[...]

    def hidden_step(i, carry):
        for t in range(16):
            b = i * 16 + t
            span = pl.ds(pl.multiple_of(b * BLK, BLK), BLK)
            nodes = feat[:, :, span].astype(f32).reshape(F, BLK).T.astype(bf16)
            feat_n[b] = nodes
            hid[b] = jnp.dot(nodes, w, preferred_element_type=f32).astype(bf16)
        return carry

    lax.fori_loop(0, BC // 16, hidden_step, 0)

    plan_copy.wait()
    tile_copy.wait()

    def forward_step(i, total):
        for t in range(UNROLL):
            p = i * UNROLL + t
            keep = plan_s[KEEP, p].astype(f32)
            total = total * keep + jnp.dot(
                tv[plan_s[ORDER, p]], hid[plan_s[TAKE, p]], preferred_element_type=f32
            )
            prods[p] = total.astype(bf16)
        return total

    lax.fori_loop(0, TILE_CAP // UNROLL, forward_step, jnp.zeros((BLK, F), f32))
    for b in range(BR):
        has = plan_s[HAS, b].astype(f32)
        sub, place = b % SUB // WIDE, b % SUB % WIDE * BLK
        block = (prods[plan_s[LAST, b]].astype(f32) * has).astype(bf16)
        part[sub, b // SUB, place : place + BLK] = block

    x = col // 2
    yl = col % 2

    def spot(dx, dy):
        return ((x + dx) % 4) * 2 + (yl + dy) % 2

    def both(q, dx):
        return part.at[q, pl.ds(((x + dx) % 4) * 2, 2)]

    def add_to(src, dst, q, index, to):
        return start_remote(
            pending, src, dst, r_send.at[index, q], r_recv.at[index, q], col=to
        )

    x_got = {}
    y_got = {}
    every = [(2, 1), (2, 0), (1, 1), (3, 1), (1, 0), (3, 0), (0, 1)]
    def first(q):
        if SUM_PATH[q] == "yx":
            for dx in (2, 1, 3, 0):
                src = part.at[q, spot(dx, 1)]
                y_got[q, dx] = add_to(src, y_in.at[q, dx], q, 4 + dx, spot(0, 1))
        elif SUM_PATH[q] == "xy":
            for dx in (2, 1, 3):
                x_got[q, dx] = add_to(both(q, dx), x_in.at[q, dx], q, dx, spot(dx, 0))
        else:
            for k, (dx, dy) in enumerate(every):
                src = part.at[q, spot(dx, dy)]
                x_got[q, k] = add_to(src, d_in.at[q, k], q, 8 + k, spot(dx, dy))

    def second(q):
        if SUM_PATH[q] == "yx":
            for dx in (2, 1, 3):
                y_got[q, dx].wait_recv()
                x_sum[q, dx] = (
                    part[q, spot(dx, 0)].astype(f32) + y_in[q, dx].astype(f32)
                ).astype(bf16)
                x_got[q, dx] = add_to(x_sum.at[q, dx], x_in.at[q, dx, 0], q, dx, spot(dx, 0))
        elif SUM_PATH[q] == "xy":
            side = part[q, spot(0, 1)].astype(f32)
            for dx in (2, 1, 3):
                x_got[q, dx].wait_recv()
                side = side + x_in[q, dx, (yl + 1) % 2].astype(f32)
            x_sum[q, 0] = side.astype(bf16)
            y_got[q, 0] = add_to(x_sum.at[q, 0], y_in.at[q, 0], q, 4, spot(0, 1))

    def summed(q):
        pre = part[q, col].astype(f32)
        if SUM_PATH[q] == "direct":
            for k in range(NCOL - 1):
                x_got[q, k].wait_recv()
                pre = pre + d_in[q, k].astype(f32)
            return pre
        for dx in (2, 1, 3):
            if SUM_PATH[q] == "yx":
                x_got[q, dx].wait_recv()
                pre = pre + x_in[q, dx, 0].astype(f32)
            else:
                pre = pre + x_in[q, dx, yl].astype(f32)
        y_got[q, 0].wait_recv()
        return pre + y_in[q, 0].astype(f32)

    gathers = {}

    def gather(dx, dy, q, tx, ty):
        piece = grad_t.at[pl.ds(spot(dx, dy) * SUB + q * WIDE, WIDE)]
        rx, ry = (dx - tx) % 4, (dy - ty) % 2
        index = rx * 2 + ry
        gathers[rx, ry, q] = start_remote(
            pending, piece, piece, g_send.at[index, q], g_recv.at[index, q], col=spot(tx, ty)
        )

    def here(dx, dy, q):
        gathers.pop((dx, dy, q)).wait_recv()

    def finish(q):
        pre = summed(q)
        sig = jax.nn.sigmoid(pre)
        span = pl.ds(q * WIDE * BLK, WIDE * BLK)
        grad = cot[span].astype(f32) * sig * (1.0 + pre * (1.0 - sig))
        for i in range(WIDE):
            block = grad[i * BLK : (i + 1) * BLK].T
            grad_t[col * SUB + q * WIDE + i] = block.astype(bf16)
        if GATHER_PATH[q] == "yx":
            ways = [(0, 1), (2, 0), (1, 0), (3, 0)]
        elif GATHER_PATH[q] == "xy":
            ways = [(2, 0), (1, 0), (3, 0), (0, 1)]
        else:
            ways = every
        for tx, ty in ways:
            gather(0, 0, q, tx, ty)
        act[span] = (pre * sig).astype(bf16)

    def spread(q):
        if GATHER_PATH[q] == "yx":
            here(0, 1, q)
            for tx in (2, 1, 3):
                gather(0, 1, q, tx, 0)
        elif GATHER_PATH[q] == "xy":
            for dx in (3, 1, 2):
                here(dx, 0, q)
                gather(dx, 0, q, 0, 1)

    def drain(q):
        got = [v for d in (x_got, y_got) for key, v in d.items() if key[0] == q]
        for copy in got:
            copy.wait_send()
            pending[:] = [other_copy for other_copy in pending if other_copy is not copy]

    steps = {"f": first, "s": second, "e": finish, "g": spread, "d": drain}
    for step in SCHEDULE.split():
        steps[step[0]](int(step[1]))
    for key in list(gathers):
        here(*key)

    def backward_step(i, total):
        for t in range(UNROLL):
            p = i * UNROLL + t
            keep = plan_s[5 + KEEP, p].astype(f32)
            total = total * keep + jnp.dot(
                grad_t[plan_s[5 + TAKE, p]], tv[plan_s[5 + ORDER, p]], preferred_element_type=f32
            )
            prods[p] = total.astype(bf16)
        return total

    lax.fori_loop(0, TILE_CAP // UNROLL, backward_step, jnp.zeros((F, BLK), f32))

    chips = [(0, 1), (0, 2), (0, 3), (1, 0), (1, 1), (1, 2), (1, 3), (0, 0)]
    pairs = {}

    def panel_step(i, total):
        for t in range(16):
            b = i * 16 + t
            has = plan_s[5 + HAS, b].astype(f32)
            block = (prods[plan_s[5 + LAST, b]].astype(f32) * has).astype(bf16)
            back[b] = block
            out = jnp.dot(w, block, preferred_element_type=f32)
            span = pl.ds(pl.multiple_of(b * BLK, BLK), BLK)
            slabs[:, :, span] = out.reshape(NROW, PER, BLK).astype(bf16)
            total = total + jnp.dot(block, feat_n[b], preferred_element_type=f32)
        return total

    def start_pairs(h, items):
        for dy, dz in items:
            k = chips.index((dy, dz))
            pairs[dy, dz, h] = start_remote(
                pending,
                half(slabs.at[at(dy, dz, other)], h),
                pbuf.at[h, k],
                p_send.at[h, k],
                p_recv.at[h, k],
                row=partner,
            )

    gw_part = lax.fori_loop(0, BC // 32, panel_step, jnp.zeros((F, F), f32))
    start_pairs(0, [(0, 2), (1, 2), (0, 1), (1, 1), (0, 3), (1, 3), (1, 0), (0, 0)])
    gw_part = lax.fori_loop(BC // 32, BC // 16, panel_step, gw_part)
    gw_part = gw_part.T
    for r in range(NROW):
        gwbuf[r % 2, r // 2] = gw_part[r * PER : (r + 1) * PER]
    gw_pair = start_remote(
        pending, gwbuf.at[other], gwpair, w_send.at[7], w_recv.at[7], row=partner
    )


    def pair_sum(dy, dz, h):
        pairs[dy, dz, h].wait_recv()
        k = chips.index((dy, dz))
        own = slabs[at(dy, dz, core), :, h * HALF : (h + 1) * HALF]
        return own.astype(f32) + pbuf[h, k].astype(f32)

    def pass_sum(value, h, k, to):
        sbuf[h, k] = value.astype(bf16)
        return start_remote(
            pending, sbuf.at[h, k], rbuf.at[h, k], s_send.at[h, k], s_recv.at[h, k], row=to
        )

    start_pairs(1, [(1, 2), (1, 1), (1, 3), (1, 0), (0, 2), (0, 1), (0, 3), (0, 0)])

    gw_pair.wait_recv()
    gwsum[...] = gwbuf[core] + gwpair[...]
    shares = []
    for k, (dy, dz) in enumerate(chips[:7]):
        chip = ((yh + dy) % 2) * 4 + (z + dz) % 4
        shares.append(
            start_remote(
                pending,
                gwsum.at[chip],
                gwrow.at[k],
                w_send.at[k],
                w_recv.at[k],
                row=at(dy, dz, core),
            )
        )

    sums = {}
    for dz in (2, 1, 3):
        for dy in (1, 0):
            k = chips.index((dy, dz))
            sums[dy, dz, 0] = pass_sum(pair_sum(dy, dz, 0), 0, k, at(0, dz, core))
    for dz in (2, 1, 3, 0):
        k = chips.index((1, dz))
        sums[1, dz, 1] = pass_sum(pair_sum(1, dz, 1), 1, k, across)

    for dz in (2, 1, 3):
        k = chips.index((0, dz))
        value = pair_sum(0, dz, 1)
        sums[1, dz, 1].wait_recv()
        value = value + rbuf[1, chips.index((1, dz))].astype(f32)
        sums[0, dz, 1] = pass_sum(value, 1, k, at(0, dz, core))

    gw_sum = gwsum[me // 2]
    for k in range(7):
        shares[k].wait_recv()
        gw_sum = gw_sum + gwrow[k]
    gwmine[...] = gw_sum
    spreads = []
    for k in range(1, NCOL):
        spreads.append(
            start_remote(
                pending, gwmine, gwcol.at[k], c_send.at[k], c_recv.at[k], col=cpeers[k - 1]
            )
        )

    value = pair_sum(1, 0, 0)
    for dz in (1, 2, 3):
        sums[1, dz, 0].wait_recv()
        value = value + rbuf[0, chips.index((1, dz))].astype(f32)
    sums[1, 0, 0] = pass_sum(value, 0, chips.index((1, 0)), across)

    total = pair_sum(0, 0, 1)
    sums[1, 0, 1].wait_recv()
    total = total + rbuf[1, chips.index((1, 0))].astype(f32)
    for dz in (1, 2, 3):
        sums[0, dz, 1].wait_recv()
        total = total + rbuf[1, chips.index((0, dz))].astype(f32)
    gf[:, HALF:] = total.astype(bf16)

    total = pair_sum(0, 0, 0)
    for dy, dz in ((0, 1), (0, 2), (0, 3), (1, 0)):
        sums[dy, dz, 0].wait_recv()
        total = total + rbuf[0, chips.index((dy, dz))].astype(f32)
    gf[:, :HALF] = total.astype(bf16)

    for k in range(1, NCOL):
        spreads[k - 1].wait_recv()
        gw_sum = gw_sum + gwcol[k]
    gw[...] = gw_sum
    for copy in pending:
        copy.wait_send()


def write_kernel(act, gw, gf, act_out, gw_out, gf_out, act_v, gw_v, gf_v, sem):
    def copies(ends, base):
        return [
            pltpu.make_async_copy(src, dst, sem.at[base + i]) for i, (src, dst) in enumerate(ends)
        ]

    reads = copies([(gf, gf_v), (act, act_v), (gw, gw_v)], 0)
    writes = copies([(gf_v, gf_out), (act_v, act_out), (gw_v, gw_out)], 3)
    for copy in reads:
        copy.start()
    for read, write in zip(reads, writes):
        read.wait()
        write.start()
    for copy in writes:
        copy.wait()


def dma(*shape):
    return pltpu.SemaphoreType.DMA(shape)


def on_device(features, weight, tiles, tile_rows, tile_cols, tile_count, cotangent):
    sds = jax.ShapeDtypeStruct
    shapes = (sds((CHUNK, F), bf16), sds((PER, F), f32), sds((PER, PANEL), bf16))
    outs = pl.pallas_call(
        layer_kernel,
        out_shape=shapes,
        in_specs=[any_spec()] * 7,
        out_specs=(vmem_spec(), vmem_spec(), vmem_spec()),
        scratch_shapes=[
            pltpu.VMEM((F, F), bf16),
            pltpu.VMEM((1, TILE_CAP), i32),
            pltpu.VMEM((1, TILE_CAP), i32),
            pltpu.VMEM((1, 1), i32),
            pltpu.VMEM((CHUNK, F), bf16),
            pltpu.VMEM((TILE_CAP, BLK, BLK), bf16),
            pltpu.VMEM((NROW, PER, PANEL), bf16),
            pltpu.VMEM((BC, BLK, F), bf16),
            pltpu.VMEM((BC, BLK, F), bf16),
            pltpu.VMEM((TILE_CAP, BLK, BLK), bf16),
            pltpu.VMEM((NSUB, NCOL, WIDE * BLK, F), bf16),
            pltpu.VMEM((NSUB, 4, WIDE * BLK, F), bf16),
            pltpu.VMEM((NSUB, 4, 2, WIDE * BLK, F), bf16),
            pltpu.VMEM((NSUB, 4, WIDE * BLK, F), bf16),
            pltpu.VMEM((NSUB, NCOL - 1, WIDE * BLK, F), bf16),
            pltpu.VMEM((BR, F, BLK), bf16),
            pltpu.VMEM((BC, F, BLK), bf16),
            pltpu.VMEM((NROW, PER, PANEL), bf16),
            pltpu.VMEM((2, 8, PER, HALF), bf16),
            pltpu.VMEM((2, 7, PER, HALF), bf16),
            pltpu.VMEM((2, 7, PER, HALF), bf16),
            pltpu.VMEM((2, 8, PER, F), f32),
            pltpu.VMEM((8, PER, F), f32),
            pltpu.VMEM((8, PER, F), f32),
            pltpu.VMEM((7, PER, F), f32),
            pltpu.VMEM((PER, F), f32),
            pltpu.VMEM((NCOL, PER, F), f32),
            pltpu.VMEM((16, TILE_CAP), i32),
            pltpu.SMEM((16, TILE_CAP), i32),
            dma(8), dma(16), dma(16), dma(15), dma(15),
            dma(16, NSUB), dma(16, NSUB), dma(NCOL, NSUB), dma(NCOL, NSUB),
            dma(2, 8), dma(2, 8), dma(2, 7), dma(2, 7), dma(8), dma(8),
            dma(NCOL), dma(NCOL),
        ],
        compiler_params=pltpu.CompilerParams(
            collective_id=0, has_side_effects=True, vmem_limit_bytes=60 * MIB
        ),
        cost_estimate=pl.CostEstimate(
            flops=4 * TILE_CAP * BLK**3, bytes_accessed=11 * MIB, transcendentals=CHUNK * F
        ),
        name="graph_layer",
    )(features.T, weight, tiles, tile_rows[0], tile_cols[0], tile_count, cotangent)
    activated, grad_weight, gf_t = pl.pallas_call(
        write_kernel,
        out_shape=shapes,
        in_specs=[any_spec()] * 3,
        out_specs=(any_spec(),) * 3,
        scratch_shapes=[pltpu.VMEM(x.shape, x.dtype) for x in shapes] + [dma(6)],
        compiler_params=pltpu.CompilerParams(vmem_limit_bytes=60 * MIB),
        name="write_results",
    )(*outs)
    return (activated, grad_weight, gf_t.T)


def solution(mesh):
    return jax.shard_map(
        on_device,
        mesh=mesh,
        in_specs=(
            P("col", "row"),
            P(),
            P("row", "col", None, None, None),
            P("row", "col", None),
            P("row", "col", None),
            P("row", "col"),
            P(("row", "col"), None),
        ),
        out_specs=(P(("row", "col"), None), P("row", None), P("col", "row")),
        check_vma=False,
    )
```

```python
import jax
import jax.numpy as jnp
from jax import lax
from jax.experimental import pallas as pl
from jax.experimental.pallas import tpu as pltpu
from jax.sharding import PartitionSpec as P

F = 128
BLK = 128
NROW = 16
NCOL = 8
BR = 32
BC = 64
TILE_CAP = 256
PANEL = BC * BLK
HALF = PANEL // 2
CHUNK = 512
SUB = CHUNK // BLK
PER = F // NROW
UNROLL = 128
MIB = 1024 * 1024
MESH = pl.DeviceIdType.MESH

f32 = jnp.float32
bf16 = jnp.bfloat16
i32 = jnp.int32

NSUB = 4
WIDE = SUB // NSUB
SUM_PATH = ("yx", "xy", "yx", "xy")
GATHER_PATH = ("xy", "yx", "xy", "yx")
SCHEDULE = "f0 f1 f2 f3 s0 s1 s2 s3 e0 e1 e2 e3 g0 g1 g2 g3"

ORDER, TAKE, KEEP, LAST, HAS = range(5)


def any_spec():
    return pl.BlockSpec(memory_space=pl.ANY)


def start_remote(pending, src, dst, send, recv, **where):
    copy = pltpu.make_async_remote_copy(
        src_ref=src,
        dst_ref=dst,
        send_sem=send,
        recv_sem=recv,
        device_id=where,
        device_id_type=MESH,
    )
    copy.start()
    pending.append(copy)
    return copy


def make_plan(key_block, take, live, dead_block):
    n = TILE_CAP
    across = lax.broadcasted_iota(i32, (n, n), 1)
    down = lax.broadcasted_iota(i32, (n, n), 0)
    block = jnp.where(live, key_block, dead_block)
    block_r = jnp.broadcast_to(block, (n, n))
    block_c = block_r.T
    key_r = block_r * n + across
    key_c = block_c * n + down
    rank = jnp.sum(jnp.where(key_c < key_r, 1, 0), axis=0, keepdims=True)
    rank_c = jnp.broadcast_to(rank, (n, n)).T
    take_c = jnp.broadcast_to(take, (n, n)).T
    hit = rank_c == across
    order = jnp.sum(jnp.where(hit, down, 0), axis=0, keepdims=True)
    taken = jnp.sum(jnp.where(hit, take_c, 0), axis=0, keepdims=True)
    mine = jnp.sum(jnp.where(hit, block_c, 0), axis=0, keepdims=True)
    before = jnp.sum(jnp.where(rank_c == across - 1, block_c, 0), axis=0, keepdims=True)
    first = lax.broadcasted_iota(i32, (1, n), 1) == 0
    keep = jnp.where(first | (mine != before), 0, 1)
    last = jnp.maximum(jnp.sum(jnp.where(block_c <= across, 1, 0), axis=0, keepdims=True) - 1, 0)
    has = jnp.where(jnp.sum(jnp.where(block_c == across, 1, 0), axis=0, keepdims=True) > 0, 1, 0)
    return [order, taken, keep, last, has]


def layer_kernel(
    feat_in, weight_in, tiles, rows_in, cols_in, count_in, cot_in,
    act_out, gw_out, gf_out,
    act, gw, gf, weight, rows_v, cols_v, count_v, cot,
    tv, feat, feat_n, hid, prods, part, x_sum, x_in, y_in, d_in, grad_t,
    back, slabs, pbuf, sbuf, rbuf, gwbuf, gwpair, gwsum, gwrow, gwmine, gwcol, plan_v, plan_s,
    l_sem, a_send, a_recv, f_send, f_recv, r_send, r_recv, g_send, g_recv,
    p_send, p_recv, s_send, s_recv, w_send, w_recv, c_send, c_recv,
):
    me = lax.axis_index("row")
    col = lax.axis_index("col")
    yh = me // 8
    z = (me // 2) % 4
    core = me % 2
    other = 1 - core

    def at(dy, dz, k):
        return ((yh + dy) % 2) * 8 + ((z + dz) % 4) * 2 + k

    partner = at(0, 0, other)
    across = at(1, 0, core)
    peers = [partner] + [at(dy, dz, core) for dy in (0, 1) for dz in range(4) if dy + dz]
    cpeers = [(col + k) % NCOL for k in range(1, NCOL)]

    tile_copy = pltpu.make_async_copy(tiles.at[0, 0], tv, l_sem.at[0])
    tile_copy.start()
    own_copy = pltpu.make_async_copy(feat_in, feat.at[me], l_sem.at[1])
    own_copy.start()
    small = []
    for i, (src, dst) in enumerate(
        [(rows_in, rows_v), (cols_in, cols_v), (count_in, count_v), (weight_in, weight), (cot_in, cot)]
    ):
        copy = pltpu.make_async_copy(src, dst, l_sem.at[3 + i])
        copy.start()
        small.append(copy)

    barrier = pltpu.get_barrier_semaphore()
    for r in peers:
        pl.semaphore_signal(barrier, inc=1, device_id={"row": r}, device_id_type=MESH)
    for c in cpeers:
        pl.semaphore_signal(barrier, inc=1, device_id={"col": c}, device_id_type=MESH)
    pl.semaphore_wait(barrier, len(peers) + len(cpeers))

    pending = []

    def half(ref, h):
        return ref.at[:, pl.ds(h * HALF, HALF)]

    got = {}

    def send(dy, dz, h, ty, tz):
        piece = half(feat.at[at(dy, dz, core)], h)
        src = half(feat_in, h) if (dy, dz) == (0, 0) else piece
        ry, rz = (dy - ty) % 2, (dz - tz) % 4
        index = h * 8 + ry * 4 + rz
        got[ry, rz, h] = start_remote(
            pending, src, piece, a_send.at[index], a_recv.at[index], row=at(ty, tz, core)
        )

    send(0, 0, 1, 1, 0)
    for tz in (2, 1, 3):
        send(0, 0, 0, 0, tz)
    send(0, 0, 0, 1, 0)
    for tz in (2, 1, 3):
        send(0, 0, 1, 0, tz)
    own_hand = start_remote(
        pending, feat_in, feat.at[me], f_send.at[0], f_recv.at[0], row=partner
    )

    for copy in small:
        copy.wait()
    live = lax.broadcasted_iota(i32, (1, TILE_CAP), 1) < count_v[0, 0]
    forward = make_plan(rows_v[...], cols_v[...], live, BR)
    backward = make_plan(cols_v[...], rows_v[...], live, BC)
    for i, line in enumerate(forward + backward):
        plan_v[i : i + 1, :] = line
    plan_copy = pltpu.make_async_copy(plan_v, plan_s, l_sem.at[2])
    plan_copy.start()

    handed = [own_hand]

    def hand(dy, dz, h):
        index = len(handed)
        piece = half(feat.at[at(dy, dz, core)], h)
        handed.append(
            start_remote(
                pending, piece, piece, f_send.at[index], f_recv.at[index], row=partner
            )
        )

    got[1, 0, 1].wait_recv()
    for tz in (2, 1, 3):
        send(1, 0, 1, 0, tz)
    hand(1, 0, 1)
    for dz in (1, 3, 2):
        got[0, dz, 0].wait_recv()
        send(0, dz, 0, 1, 0)
        hand(0, dz, 0)
    for dy, dz, h in (
        (1, 0, 0), (0, 1, 1), (0, 3, 1), (0, 2, 1), (1, 1, 0), (1, 3, 0), (1, 2, 0),
        (1, 1, 1), (1, 3, 1), (1, 2, 1),
    ):
        got[dy, dz, h].wait_recv()
        hand(dy, dz, h)
    own_copy.wait()
    for copy in handed:
        copy.wait_recv()

    w = weight[...]

    def hidden_step(i, carry):
        for t in range(16):
            b = i * 16 + t
            span = pl.ds(pl.multiple_of(b * BLK, BLK), BLK)
            nodes = feat[:, :, span].astype(f32).reshape(F, BLK).T.astype(bf16)
            feat_n[b] = nodes
            hid[b] = jnp.dot(nodes, w, preferred_element_type=f32).astype(bf16)
        return carry

    lax.fori_loop(0, BC // 16, hidden_step, 0)

    plan_copy.wait()
    tile_copy.wait()

    def forward_step(i, total):
        for t in range(UNROLL):
            p = i * UNROLL + t
            keep = plan_s[KEEP, p].astype(f32)
            total = total * keep + jnp.dot(
                tv[plan_s[ORDER, p]], hid[plan_s[TAKE, p]], preferred_element_type=f32
            )
            prods[p] = total.astype(bf16)
        return total

    lax.fori_loop(0, TILE_CAP // UNROLL, forward_step, jnp.zeros((BLK, F), f32))
    for b in range(BR):
        has = plan_s[HAS, b].astype(f32)
        sub, place = b % SUB // WIDE, b % SUB % WIDE * BLK
        block = (prods[plan_s[LAST, b]].astype(f32) * has).astype(bf16)
        part[sub, b // SUB, place : place + BLK] = block

    x = col // 2
    yl = col % 2

    def spot(dx, dy):
        return ((x + dx) % 4) * 2 + (yl + dy) % 2

    def both(q, dx):
        return part.at[q, pl.ds(((x + dx) % 4) * 2, 2)]

    def add_to(src, dst, q, index, to):
        return start_remote(
            pending, src, dst, r_send.at[index, q], r_recv.at[index, q], col=to
        )

    x_got = {}
    y_got = {}
    every = [(2, 1), (2, 0), (1, 1), (3, 1), (1, 0), (3, 0), (0, 1)]
    def first(q):
        if SUM_PATH[q] == "yx":
            for dx in (2, 1, 3, 0):
                src = part.at[q, spot(dx, 1)]
                y_got[q, dx] = add_to(src, y_in.at[q, dx], q, 4 + dx, spot(0, 1))
        elif SUM_PATH[q] == "xy":
            for dx in (2, 1, 3):
                x_got[q, dx] = add_to(both(q, dx), x_in.at[q, dx], q, dx, spot(dx, 0))
        else:
            for k, (dx, dy) in enumerate(every):
                src = part.at[q, spot(dx, dy)]
                x_got[q, k] = add_to(src, d_in.at[q, k], q, 8 + k, spot(dx, dy))

    def second(q):
        if SUM_PATH[q] == "yx":
            for dx in (2, 1, 3):
                y_got[q, dx].wait_recv()
                x_sum[q, dx] = (
                    part[q, spot(dx, 0)].astype(f32) + y_in[q, dx].astype(f32)
                ).astype(bf16)
                x_got[q, dx] = add_to(x_sum.at[q, dx], x_in.at[q, dx, 0], q, dx, spot(dx, 0))
        elif SUM_PATH[q] == "xy":
            side = part[q, spot(0, 1)].astype(f32)
            for dx in (2, 1, 3):
                x_got[q, dx].wait_recv()
                side = side + x_in[q, dx, (yl + 1) % 2].astype(f32)
            x_sum[q, 0] = side.astype(bf16)
            y_got[q, 0] = add_to(x_sum.at[q, 0], y_in.at[q, 0], q, 4, spot(0, 1))

    def summed(q):
        pre = part[q, col].astype(f32)
        if SUM_PATH[q] == "direct":
            for k in range(NCOL - 1):
                x_got[q, k].wait_recv()
                pre = pre + d_in[q, k].astype(f32)
            return pre
        for dx in (2, 1, 3):
            if SUM_PATH[q] == "yx":
                x_got[q, dx].wait_recv()
                pre = pre + x_in[q, dx, 0].astype(f32)
            else:
                pre = pre + x_in[q, dx, yl].astype(f32)
        y_got[q, 0].wait_recv()
        return pre + y_in[q, 0].astype(f32)

    gathers = {}

    def gather(dx, dy, q, tx, ty):
        piece = grad_t.at[pl.ds(spot(dx, dy) * SUB + q * WIDE, WIDE)]
        rx, ry = (dx - tx) % 4, (dy - ty) % 2
        index = rx * 2 + ry
        gathers[rx, ry, q] = start_remote(
            pending, piece, piece, g_send.at[index, q], g_recv.at[index, q], col=spot(tx, ty)
        )

    def here(dx, dy, q):
        gathers.pop((dx, dy, q)).wait_recv()

    def finish(q):
        pre = summed(q)
        sig = jax.nn.sigmoid(pre)
        span = pl.ds(q * WIDE * BLK, WIDE * BLK)
        grad = cot[span].astype(f32) * sig * (1.0 + pre * (1.0 - sig))
        for i in range(WIDE):
            block = grad[i * BLK : (i + 1) * BLK].T
            grad_t[col * SUB + q * WIDE + i] = block.astype(bf16)
        if GATHER_PATH[q] == "yx":
            ways = [(0, 1), (2, 0), (1, 0), (3, 0)]
        elif GATHER_PATH[q] == "xy":
            ways = [(2, 0), (1, 0), (3, 0), (0, 1)]
        else:
            ways = every
        for tx, ty in ways:
            gather(0, 0, q, tx, ty)
        act[span] = (pre * sig).astype(bf16)

    def spread(q):
        if GATHER_PATH[q] == "yx":
            here(0, 1, q)
            for tx in (2, 1, 3):
                gather(0, 1, q, tx, 0)
        elif GATHER_PATH[q] == "xy":
            for dx in (3, 1, 2):
                here(dx, 0, q)
                gather(dx, 0, q, 0, 1)

    def drain(q):
        got = [v for d in (x_got, y_got) for key, v in d.items() if key[0] == q]
        for copy in got:
            copy.wait_send()
            pending[:] = [other_copy for other_copy in pending if other_copy is not copy]

    steps = {"f": first, "s": second, "e": finish, "g": spread, "d": drain}
    for step in SCHEDULE.split():
        steps[step[0]](int(step[1]))
    act_copy = pltpu.make_async_copy(act, act_out, l_sem.at[8])
    act_copy.start()
    for key in list(gathers):
        here(*key)

    def backward_step(i, total):
        for t in range(UNROLL):
            p = i * UNROLL + t
            keep = plan_s[5 + KEEP, p].astype(f32)
            total = total * keep + jnp.dot(
                grad_t[plan_s[5 + TAKE, p]], tv[plan_s[5 + ORDER, p]], preferred_element_type=f32
            )
            prods[p] = total.astype(bf16)
        return total

    lax.fori_loop(0, TILE_CAP // UNROLL, backward_step, jnp.zeros((F, BLK), f32))

    chips = [(0, 1), (0, 2), (0, 3), (1, 0), (1, 1), (1, 2), (1, 3), (0, 0)]
    pairs = {}

    def panel_step(i, total):
        for t in range(16):
            b = i * 16 + t
            has = plan_s[5 + HAS, b].astype(f32)
            block = (prods[plan_s[5 + LAST, b]].astype(f32) * has).astype(bf16)
            back[b] = block
            out = jnp.dot(w, block, preferred_element_type=f32)
            span = pl.ds(pl.multiple_of(b * BLK, BLK), BLK)
            slabs[:, :, :, span] = out.reshape(NROW // 2, 2, PER, BLK).astype(bf16)
            total = total + jnp.dot(block, feat_n[b], preferred_element_type=f32)
        return total

    def start_pairs(h):
        pairs[h] = start_remote(
            pending,
            slabs.at[:, other, :, pl.ds(h * HALF, HALF)],
            pbuf.at[h],
            p_send.at[h],
            p_recv.at[h],
            row=partner,
        )

    gw_part = lax.fori_loop(0, BC // 32, panel_step, jnp.zeros((F, F), f32))
    start_pairs(0)
    gw_part = lax.fori_loop(BC // 32, BC // 16, panel_step, gw_part)
    gw_part = gw_part.T
    for r in range(NROW):
        gwbuf[r % 2, r // 2] = gw_part[r * PER : (r + 1) * PER]
    gw_pair = start_remote(
        pending, gwbuf.at[other], gwpair, w_send.at[7], w_recv.at[7], row=partner
    )


    def pair_sum(dy, dz, h):
        if h in pairs:
            pairs.pop(h).wait_recv()
        chip = ((yh + dy) % 2) * 4 + (z + dz) % 4
        own = slabs[chip, core, :, h * HALF : (h + 1) * HALF]
        return own.astype(f32) + pbuf[h, chip].astype(f32)

    def pass_sum(value, h, k, to):
        sbuf[h, k] = value.astype(bf16)
        return start_remote(
            pending, sbuf.at[h, k], rbuf.at[h, k], s_send.at[h, k], s_recv.at[h, k], row=to
        )

    start_pairs(1)

    gw_pair.wait_recv()
    gwsum[...] = gwbuf[core] + gwpair[...]
    shares = []
    for k, (dy, dz) in enumerate(chips[:7]):
        chip = ((yh + dy) % 2) * 4 + (z + dz) % 4
        shares.append(
            start_remote(
                pending,
                gwsum.at[chip],
                gwrow.at[k],
                w_send.at[k],
                w_recv.at[k],
                row=at(dy, dz, core),
            )
        )

    sums = {}
    for dz in (2, 1, 3):
        for dy in (1, 0):
            k = chips.index((dy, dz))
            sums[dy, dz, 0] = pass_sum(pair_sum(dy, dz, 0), 0, k, at(0, dz, core))
    for dz in (2, 1, 3, 0):
        k = chips.index((1, dz))
        sums[1, dz, 1] = pass_sum(pair_sum(1, dz, 1), 1, k, across)

    for dz in (2, 1, 3):
        k = chips.index((0, dz))
        value = pair_sum(0, dz, 1)
        sums[1, dz, 1].wait_recv()
        value = value + rbuf[1, chips.index((1, dz))].astype(f32)
        sums[0, dz, 1] = pass_sum(value, 1, k, at(0, dz, core))

    gw_sum = gwsum[me // 2]
    for k in range(7):
        shares[k].wait_recv()
        gw_sum = gw_sum + gwrow[k]
    gwmine[...] = gw_sum
    spreads = []
    for k in range(1, NCOL):
        spreads.append(
            start_remote(
                pending, gwmine, gwcol.at[k], c_send.at[k], c_recv.at[k], col=cpeers[k - 1]
            )
        )

    value = pair_sum(1, 0, 0)
    for dz in (1, 2, 3):
        sums[1, dz, 0].wait_recv()
        value = value + rbuf[0, chips.index((1, dz))].astype(f32)
    sums[1, 0, 0] = pass_sum(value, 0, chips.index((1, 0)), across)

    total = pair_sum(0, 0, 1)
    sums[1, 0, 1].wait_recv()
    total = total + rbuf[1, chips.index((1, 0))].astype(f32)
    for dz in (1, 2, 3):
        sums[0, dz, 1].wait_recv()
        total = total + rbuf[1, chips.index((0, dz))].astype(f32)
    gf[:, HALF:] = total.astype(bf16)
    outs = [act_copy, pltpu.make_async_copy(half(gf, 1), half(gf_out, 1), l_sem.at[9])]
    outs[1].start()

    total = pair_sum(0, 0, 0)
    for dy, dz in ((0, 1), (0, 2), (0, 3), (1, 0)):
        sums[dy, dz, 0].wait_recv()
        total = total + rbuf[0, chips.index((dy, dz))].astype(f32)
    gf[:, :HALF] = total.astype(bf16)
    outs.append(pltpu.make_async_copy(half(gf, 0), half(gf_out, 0), l_sem.at[10]))
    outs[2].start()

    for k in range(1, NCOL):
        spreads[k - 1].wait_recv()
        gw_sum = gw_sum + gwcol[k]
    gw[...] = gw_sum
    outs.append(pltpu.make_async_copy(gw, gw_out, l_sem.at[11]))
    outs[3].start()
    for copy in pending:
        copy.wait_send()
    for copy in outs:
        copy.wait()


def write_kernel(act, gw, gf, act_out, gw_out, gf_out, act_v, gw_v, gf_v, sem):
    def copies(ends, base):
        return [
            pltpu.make_async_copy(src, dst, sem.at[base + i]) for i, (src, dst) in enumerate(ends)
        ]

    reads = copies([(gf, gf_v), (act, act_v), (gw, gw_v)], 0)
    writes = copies([(gf_v, gf_out), (act_v, act_out), (gw_v, gw_out)], 3)
    for copy in reads:
        copy.start()
    for read, write in zip(reads, writes):
        read.wait()
        write.start()
    for copy in writes:
        copy.wait()


def dma(*shape):
    return pltpu.SemaphoreType.DMA(shape)


def on_device(features, weight, tiles, tile_rows, tile_cols, tile_count, cotangent):
    sds = jax.ShapeDtypeStruct
    shapes = (sds((CHUNK, F), bf16), sds((PER, F), f32), sds((PER, PANEL), bf16))
    outs = pl.pallas_call(
        layer_kernel,
        out_shape=shapes,
        in_specs=[any_spec()] * 7,
        out_specs=(any_spec(),) * 3,
        scratch_shapes=[
            *(pltpu.VMEM(x.shape, x.dtype) for x in shapes),
            pltpu.VMEM((F, F), bf16),
            pltpu.VMEM((1, TILE_CAP), i32),
            pltpu.VMEM((1, TILE_CAP), i32),
            pltpu.VMEM((1, 1), i32),
            pltpu.VMEM((CHUNK, F), bf16),
            pltpu.VMEM((TILE_CAP, BLK, BLK), bf16),
            pltpu.VMEM((NROW, PER, PANEL), bf16),
            pltpu.VMEM((BC, BLK, F), bf16),
            pltpu.VMEM((BC, BLK, F), bf16),
            pltpu.VMEM((TILE_CAP, BLK, BLK), bf16),
            pltpu.VMEM((NSUB, NCOL, WIDE * BLK, F), bf16),
            pltpu.VMEM((NSUB, 4, WIDE * BLK, F), bf16),
            pltpu.VMEM((NSUB, 4, 2, WIDE * BLK, F), bf16),
            pltpu.VMEM((NSUB, 4, WIDE * BLK, F), bf16),
            pltpu.VMEM((NSUB, NCOL - 1, WIDE * BLK, F), bf16),
            pltpu.VMEM((BR, F, BLK), bf16),
            pltpu.VMEM((BC, F, BLK), bf16),
            pltpu.VMEM((NROW // 2, 2, PER, PANEL), bf16),
            pltpu.VMEM((2, 8, PER, HALF), bf16),
            pltpu.VMEM((2, 7, PER, HALF), bf16),
            pltpu.VMEM((2, 7, PER, HALF), bf16),
            pltpu.VMEM((2, 8, PER, F), f32),
            pltpu.VMEM((8, PER, F), f32),
            pltpu.VMEM((8, PER, F), f32),
            pltpu.VMEM((7, PER, F), f32),
            pltpu.VMEM((PER, F), f32),
            pltpu.VMEM((NCOL, PER, F), f32),
            pltpu.VMEM((16, TILE_CAP), i32),
            pltpu.SMEM((16, TILE_CAP), i32),
            dma(12), dma(16), dma(16), dma(15), dma(15),
            dma(16, NSUB), dma(16, NSUB), dma(NCOL, NSUB), dma(NCOL, NSUB),
            dma(2), dma(2), dma(2, 7), dma(2, 7), dma(8), dma(8),
            dma(NCOL), dma(NCOL),
        ],
        compiler_params=pltpu.CompilerParams(
            collective_id=0, has_side_effects=True, vmem_limit_bytes=60 * MIB
        ),
        cost_estimate=pl.CostEstimate(
            flops=4 * TILE_CAP * BLK**3, bytes_accessed=11 * MIB, transcendentals=CHUNK * F
        ),
        name="graph_layer",
    )(features.T, weight, tiles, tile_rows[0], tile_cols[0], tile_count, cotangent)
    activated, grad_weight, gf_t = pl.pallas_call(
        write_kernel,
        out_shape=shapes,
        in_specs=[any_spec()] * 3,
        out_specs=(any_spec(),) * 3,
        scratch_shapes=[pltpu.VMEM(x.shape, x.dtype) for x in shapes] + [dma(6)],
        compiler_params=pltpu.CompilerParams(vmem_limit_bytes=60 * MIB),
        name="write_results",
    )(*outs)
    return (activated, grad_weight, gf_t.T)


def solution(mesh):
    return jax.shard_map(
        on_device,
        mesh=mesh,
        in_specs=(
            P("col", "row"),
            P(),
            P("row", "col", None, None, None),
            P("row", "col", None),
            P("row", "col", None),
            P("row", "col"),
            P(("row", "col"), None),
        ),
        out_specs=(P(("row", "col"), None), P("row", None), P("col", "row")),
        check_vma=False,
    )
```

```python
import jax
import jax.numpy as jnp
from jax import lax
from jax.experimental import pallas as pl
from jax.experimental.pallas import tpu as pltpu
from jax.sharding import PartitionSpec as P

F = 128
BLK = 128
NROW = 16
NCOL = 8
BR = 32
BC = 64
TILE_CAP = 256
PANEL = BC * BLK
HALF = PANEL // 2
CHUNK = 512
SUB = CHUNK // BLK
PER = F // NROW
UNROLL = 128
MIB = 1024 * 1024
MESH = pl.DeviceIdType.MESH

f32 = jnp.float32
bf16 = jnp.bfloat16
i32 = jnp.int32

NSUB = 4
WIDE = SUB // NSUB
SUM_PATH = ("yx", "xy", "yx", "xy")
GATHER_PATH = ("xy", "yx", "xy", "yx")
SCHEDULE = "f0 f1 f2 f3 s0 s1 s2 s3 e0 e1 e2 e3 g0 g1 g2 g3"

ORDER, TAKE, KEEP, LAST, HAS = range(5)


def any_spec():
    return pl.BlockSpec(memory_space=pl.ANY)


def start_remote(pending, src, dst, send, recv, **where):
    copy = pltpu.make_async_remote_copy(
        src_ref=src,
        dst_ref=dst,
        send_sem=send,
        recv_sem=recv,
        device_id=where,
        device_id_type=MESH,
    )
    copy.start()
    pending.append(copy)
    return copy


def make_plan(key_block, take, live, dead_block):
    n = TILE_CAP
    across = lax.broadcasted_iota(i32, (n, n), 1)
    down = lax.broadcasted_iota(i32, (n, n), 0)
    block = jnp.where(live, key_block, dead_block)
    block_r = jnp.broadcast_to(block, (n, n))
    block_c = block_r.T
    key_r = block_r * n + across
    key_c = block_c * n + down
    rank = jnp.sum(jnp.where(key_c < key_r, 1, 0), axis=0, keepdims=True)
    rank_c = jnp.broadcast_to(rank, (n, n)).T
    take_c = jnp.broadcast_to(take, (n, n)).T
    hit = rank_c == across
    order = jnp.sum(jnp.where(hit, down, 0), axis=0, keepdims=True)
    taken = jnp.sum(jnp.where(hit, take_c, 0), axis=0, keepdims=True)
    mine = jnp.sum(jnp.where(hit, block_c, 0), axis=0, keepdims=True)
    before = jnp.sum(jnp.where(rank_c == across - 1, block_c, 0), axis=0, keepdims=True)
    first = lax.broadcasted_iota(i32, (1, n), 1) == 0
    keep = jnp.where(first | (mine != before), 0, 1)
    last = jnp.maximum(jnp.sum(jnp.where(block_c <= across, 1, 0), axis=0, keepdims=True) - 1, 0)
    has = jnp.where(jnp.sum(jnp.where(block_c == across, 1, 0), axis=0, keepdims=True) > 0, 1, 0)
    return [order, taken, keep, last, has]


def layer_kernel(
    feat_in, weight_in, tiles, rows_in, cols_in, count_in, cot_in,
    act_out, gw_out, gf_out,
    act, gw, gf, weight, rows_v, cols_v, count_v, cot,
    tv, feat, feat_n, hid, prods, part, x_sum, x_in, y_in, d_in, grad_t,
    back, slabs, pbuf, sbuf, rbuf, gwbuf, gwpair, gwsum, gwrow, gwmine, gwcol, plan_v, plan_s,
    l_sem, a_send, a_recv, f_send, f_recv, r_send, r_recv, g_send, g_recv,
    p_send, p_recv, s_send, s_recv, w_send, w_recv, c_send, c_recv,
):
    me = lax.axis_index("row")
    col = lax.axis_index("col")
    yh = me // 8
    z = (me // 2) % 4
    core = me % 2
    other = 1 - core

    def at(dy, dz, k):
        return ((yh + dy) % 2) * 8 + ((z + dz) % 4) * 2 + k

    partner = at(0, 0, other)
    across = at(1, 0, core)
    peers = [partner] + [at(dy, dz, core) for dy in (0, 1) for dz in range(4) if dy + dz]
    cpeers = [(col + k) % NCOL for k in range(1, NCOL)]

    tile_copy = pltpu.make_async_copy(tiles.at[0, 0], tv, l_sem.at[0])
    tile_copy.start()
    own_copy = pltpu.make_async_copy(feat_in, feat.at[me], l_sem.at[1])
    own_copy.start()
    small = []
    for i, (src, dst) in enumerate(
        [(rows_in, rows_v), (cols_in, cols_v), (count_in, count_v), (weight_in, weight), (cot_in, cot)]
    ):
        copy = pltpu.make_async_copy(src, dst, l_sem.at[3 + i])
        copy.start()
        small.append(copy)

    barrier = pltpu.get_barrier_semaphore()
    for r in peers:
        pl.semaphore_signal(barrier, inc=1, device_id={"row": r}, device_id_type=MESH)
    for c in cpeers:
        pl.semaphore_signal(barrier, inc=1, device_id={"col": c}, device_id_type=MESH)
    pl.semaphore_wait(barrier, len(peers) + len(cpeers))

    pending = []

    def half(ref, h):
        return ref.at[:, pl.ds(h * HALF, HALF)]

    got = {}

    def send(dy, dz, h, ty, tz):
        piece = half(feat.at[at(dy, dz, core)], h)
        src = half(feat_in, h) if (dy, dz) == (0, 0) else piece
        ry, rz = (dy - ty) % 2, (dz - tz) % 4
        index = h * 8 + ry * 4 + rz
        got[ry, rz, h] = start_remote(
            pending, src, piece, a_send.at[index], a_recv.at[index], row=at(ty, tz, core)
        )

    send(0, 0, 1, 1, 0)
    for tz in (2, 1, 3):
        send(0, 0, 0, 0, tz)
    send(0, 0, 0, 1, 0)
    for tz in (2, 1, 3):
        send(0, 0, 1, 0, tz)
    own_hand = start_remote(
        pending, feat_in, feat.at[me], f_send.at[0], f_recv.at[0], row=partner
    )

    for copy in small:
        copy.wait()
    live = lax.broadcasted_iota(i32, (1, TILE_CAP), 1) < count_v[0, 0]
    forward = make_plan(rows_v[...], cols_v[...], live, BR)
    backward = make_plan(cols_v[...], rows_v[...], live, BC)
    for i, line in enumerate(forward + backward):
        plan_v[i : i + 1, :] = line
    plan_copy = pltpu.make_async_copy(plan_v, plan_s, l_sem.at[2])
    plan_copy.start()

    handed = [own_hand]

    def hand(dy, dz, h):
        index = len(handed)
        piece = half(feat.at[at(dy, dz, core)], h)
        handed.append(
            start_remote(
                pending, piece, piece, f_send.at[index], f_recv.at[index], row=partner
            )
        )

    got[1, 0, 1].wait_recv()
    for tz in (2, 1, 3):
        send(1, 0, 1, 0, tz)
    hand(1, 0, 1)
    for dz in (1, 3, 2):
        got[0, dz, 0].wait_recv()
        send(0, dz, 0, 1, 0)
        hand(0, dz, 0)
    for dy, dz, h in (
        (1, 0, 0), (0, 1, 1), (0, 3, 1), (0, 2, 1), (1, 1, 0), (1, 3, 0), (1, 2, 0),
        (1, 1, 1), (1, 3, 1), (1, 2, 1),
    ):
        got[dy, dz, h].wait_recv()
        hand(dy, dz, h)
    own_copy.wait()
    for copy in handed:
        copy.wait_recv()

    w = weight[...]

    def hidden_step(i, carry):
        for t in range(16):
            b = i * 16 + t
            span = pl.ds(pl.multiple_of(b * BLK, BLK), BLK)
            nodes = feat[:, :, span].astype(f32).reshape(F, BLK).T.astype(bf16)
            feat_n[b] = nodes
            hid[b] = jnp.dot(nodes, w, preferred_element_type=f32).astype(bf16)
        return carry

    lax.fori_loop(0, BC // 16, hidden_step, 0)

    plan_copy.wait()
    tile_copy.wait()

    def forward_step(i, total):
        for t in range(UNROLL):
            p = i * UNROLL + t
            keep = plan_s[KEEP, p].astype(f32)
            total = total * keep + jnp.dot(
                tv[plan_s[ORDER, p]], hid[plan_s[TAKE, p]], preferred_element_type=f32
            )
            prods[p] = total.astype(bf16)
        return total

    lax.fori_loop(0, TILE_CAP // UNROLL, forward_step, jnp.zeros((BLK, F), f32))
    for b in range(BR):
        has = plan_s[HAS, b].astype(f32)
        sub, place = b % SUB // WIDE, b % SUB % WIDE * BLK
        block = (prods[plan_s[LAST, b]].astype(f32) * has).astype(bf16)
        part[sub, b // SUB, place : place + BLK] = block

    x = col // 2
    yl = col % 2

    def spot(dx, dy):
        return ((x + dx) % 4) * 2 + (yl + dy) % 2

    def both(q, dx):
        return part.at[q, pl.ds(((x + dx) % 4) * 2, 2)]

    def add_to(src, dst, q, index, to):
        return start_remote(
            pending, src, dst, r_send.at[index, q], r_recv.at[index, q], col=to
        )

    x_got = {}
    y_got = {}
    every = [(2, 1), (2, 0), (1, 1), (3, 1), (1, 0), (3, 0), (0, 1)]
    def first(q):
        if SUM_PATH[q] == "yx":
            for dx in (2, 1, 3, 0):
                src = part.at[q, spot(dx, 1)]
                y_got[q, dx] = add_to(src, y_in.at[q, dx], q, 4 + dx, spot(0, 1))
        elif SUM_PATH[q] == "xy":
            for dx in (2, 1, 3):
                x_got[q, dx] = add_to(both(q, dx), x_in.at[q, dx], q, dx, spot(dx, 0))
        else:
            for k, (dx, dy) in enumerate(every):
                src = part.at[q, spot(dx, dy)]
                x_got[q, k] = add_to(src, d_in.at[q, k], q, 8 + k, spot(dx, dy))

    def second(q):
        if SUM_PATH[q] == "yx":
            for dx in (2, 1, 3):
                y_got[q, dx].wait_recv()
                x_sum[q, dx] = (
                    part[q, spot(dx, 0)].astype(f32) + y_in[q, dx].astype(f32)
                ).astype(bf16)
                x_got[q, dx] = add_to(x_sum.at[q, dx], x_in.at[q, dx, 0], q, dx, spot(dx, 0))
        elif SUM_PATH[q] == "xy":
            side = part[q, spot(0, 1)].astype(f32)
            for dx in (2, 1, 3):
                x_got[q, dx].wait_recv()
                side = side + x_in[q, dx, (yl + 1) % 2].astype(f32)
            x_sum[q, 0] = side.astype(bf16)
            y_got[q, 0] = add_to(x_sum.at[q, 0], y_in.at[q, 0], q, 4, spot(0, 1))

    def summed(q):
        pre = part[q, col].astype(f32)
        if SUM_PATH[q] == "direct":
            for k in range(NCOL - 1):
                x_got[q, k].wait_recv()
                pre = pre + d_in[q, k].astype(f32)
            return pre
        for dx in (2, 1, 3):
            if SUM_PATH[q] == "yx":
                x_got[q, dx].wait_recv()
                pre = pre + x_in[q, dx, 0].astype(f32)
            else:
                pre = pre + x_in[q, dx, yl].astype(f32)
        y_got[q, 0].wait_recv()
        return pre + y_in[q, 0].astype(f32)

    gathers = {}

    def gather(dx, dy, q, tx, ty):
        piece = grad_t.at[pl.ds(spot(dx, dy) * SUB + q * WIDE, WIDE)]
        rx, ry = (dx - tx) % 4, (dy - ty) % 2
        index = rx * 2 + ry
        gathers[rx, ry, q] = start_remote(
            pending, piece, piece, g_send.at[index, q], g_recv.at[index, q], col=spot(tx, ty)
        )

    def here(dx, dy, q):
        gathers.pop((dx, dy, q)).wait_recv()

    def finish(q):
        pre = summed(q)
        sig = jax.nn.sigmoid(pre)
        span = pl.ds(q * WIDE * BLK, WIDE * BLK)
        grad = cot[span].astype(f32) * sig * (1.0 + pre * (1.0 - sig))
        for i in range(WIDE):
            block = grad[i * BLK : (i + 1) * BLK].T
            grad_t[col * SUB + q * WIDE + i] = block.astype(bf16)
        if GATHER_PATH[q] == "yx":
            ways = [(0, 1), (2, 0), (1, 0), (3, 0)]
        elif GATHER_PATH[q] == "xy":
            ways = [(2, 0), (1, 0), (3, 0), (0, 1)]
        else:
            ways = every
        for tx, ty in ways:
            gather(0, 0, q, tx, ty)
        act[span] = (pre * sig).astype(bf16)

    def spread(q):
        if GATHER_PATH[q] == "yx":
            here(0, 1, q)
            for tx in (2, 1, 3):
                gather(0, 1, q, tx, 0)
        elif GATHER_PATH[q] == "xy":
            for dx in (3, 1, 2):
                here(dx, 0, q)
                gather(dx, 0, q, 0, 1)

    def drain(q):
        got = [v for d in (x_got, y_got) for key, v in d.items() if key[0] == q]
        for copy in got:
            copy.wait_send()
            pending[:] = [other_copy for other_copy in pending if other_copy is not copy]

    steps = {"f": first, "s": second, "e": finish, "g": spread, "d": drain}
    for step in SCHEDULE.split():
        steps[step[0]](int(step[1]))
    act_copy = pltpu.make_async_copy(act, act_out, l_sem.at[8])
    act_copy.start()
    for key in list(gathers):
        here(*key)

    def backward_step(i, total):
        for t in range(UNROLL):
            p = i * UNROLL + t
            keep = plan_s[5 + KEEP, p].astype(f32)
            total = total * keep + jnp.dot(
                grad_t[plan_s[5 + TAKE, p]], tv[plan_s[5 + ORDER, p]], preferred_element_type=f32
            )
            prods[p] = total.astype(bf16)
        return total

    lax.fori_loop(0, TILE_CAP // UNROLL, backward_step, jnp.zeros((F, BLK), f32))

    chips = [(0, 1), (0, 2), (0, 3), (1, 0), (1, 1), (1, 2), (1, 3), (0, 0)]
    pairs = {}

    def panel_step(i, total):
        for t in range(16):
            b = i * 16 + t
            has = plan_s[5 + HAS, b].astype(f32)
            block = (prods[plan_s[5 + LAST, b]].astype(f32) * has).astype(bf16)
            back[b] = block
            out = jnp.dot(w, block, preferred_element_type=f32)
            span = pl.ds(pl.multiple_of(b * BLK, BLK), BLK)
            slabs[:, :, :, span] = out.reshape(NROW // 2, 2, PER, BLK).astype(bf16)
            total = total + jnp.dot(block, feat_n[b], preferred_element_type=f32)
        return total

    def start_pairs(h):
        pairs[h] = start_remote(
            pending,
            slabs.at[:, other, :, pl.ds(h * HALF, HALF)],
            pbuf.at[h],
            p_send.at[h],
            p_recv.at[h],
            row=partner,
        )

    gw_part = lax.fori_loop(0, BC // 32, panel_step, jnp.zeros((F, F), f32))
    start_pairs(0)
    gw_part = lax.fori_loop(BC // 32, BC // 16, panel_step, gw_part)
    gw_part = gw_part.T
    for r in range(NROW):
        gwbuf[r % 2, r // 2] = gw_part[r * PER : (r + 1) * PER]
    gw_pair = start_remote(
        pending, gwbuf.at[other], gwpair, w_send.at[7], w_recv.at[7], row=partner
    )


    def pair_sum(dy, dz, h):
        if h in pairs:
            pairs.pop(h).wait_recv()
        chip = ((yh + dy) % 2) * 4 + (z + dz) % 4
        own = slabs[chip, core, :, h * HALF : (h + 1) * HALF]
        return own.astype(f32) + pbuf[h, chip].astype(f32)

    def pass_sum(value, h, k, to):
        sbuf[h, k] = value.astype(bf16)
        return start_remote(
            pending, sbuf.at[h, k], rbuf.at[h, k], s_send.at[h, k], s_recv.at[h, k], row=to
        )

    start_pairs(1)

    gw_pair.wait_recv()
    gwsum[...] = gwbuf[core] + gwpair[...]
    shares = []
    for k, (dy, dz) in enumerate(chips[:7]):
        chip = ((yh + dy) % 2) * 4 + (z + dz) % 4
        shares.append(
            start_remote(
                pending,
                gwsum.at[chip],
                gwrow.at[k],
                w_send.at[k],
                w_recv.at[k],
                row=at(dy, dz, core),
            )
        )

    sums = {}
    for dz in (2, 1, 3):
        for dy in (1, 0):
            k = chips.index((dy, dz))
            sums[dy, dz, 0] = pass_sum(pair_sum(dy, dz, 0), 0, k, at(0, dz, core))
    for dz in (2, 1, 3, 0):
        k = chips.index((1, dz))
        sums[1, dz, 1] = pass_sum(pair_sum(1, dz, 1), 1, k, across)

    gw_sum = gwsum[me // 2]
    for k in range(7):
        shares[k].wait_recv()
        gw_sum = gw_sum + gwrow[k]
    gwmine[...] = gw_sum
    spreads = []
    for k in range(1, NCOL):
        spreads.append(
            start_remote(
                pending, gwmine, gwcol.at[k], c_send.at[k], c_recv.at[k], col=cpeers[k - 1]
            )
        )

    for dz in (2, 1, 3):
        k = chips.index((0, dz))
        value = pair_sum(0, dz, 1)
        sums[1, dz, 1].wait_recv()
        value = value + rbuf[1, chips.index((1, dz))].astype(f32)
        sums[0, dz, 1] = pass_sum(value, 1, k, at(0, dz, core))

    value = pair_sum(1, 0, 0)
    for dz in (1, 2, 3):
        sums[1, dz, 0].wait_recv()
        value = value + rbuf[0, chips.index((1, dz))].astype(f32)
    sums[1, 0, 0] = pass_sum(value, 0, chips.index((1, 0)), across)

    total = pair_sum(0, 0, 1)
    sums[1, 0, 1].wait_recv()
    total = total + rbuf[1, chips.index((1, 0))].astype(f32)
    for dz in (1, 2, 3):
        sums[0, dz, 1].wait_recv()
        total = total + rbuf[1, chips.index((0, dz))].astype(f32)
    gf[:, HALF:] = total.astype(bf16)
    outs = [act_copy, pltpu.make_async_copy(half(gf, 1), half(gf_out, 1), l_sem.at[9])]
    outs[1].start()

    total = pair_sum(0, 0, 0)
    for dy, dz in ((0, 1), (0, 2), (0, 3), (1, 0)):
        sums[dy, dz, 0].wait_recv()
        total = total + rbuf[0, chips.index((dy, dz))].astype(f32)
    gf[:, :HALF] = total.astype(bf16)
    outs.append(pltpu.make_async_copy(half(gf, 0), half(gf_out, 0), l_sem.at[10]))
    outs[2].start()

    for k in range(1, NCOL):
        spreads[k - 1].wait_recv()
        gw_sum = gw_sum + gwcol[k]
    gw[...] = gw_sum
    outs.append(pltpu.make_async_copy(gw, gw_out, l_sem.at[11]))
    outs[3].start()
    for copy in pending:
        copy.wait_send()
    for copy in outs:
        copy.wait()


def write_kernel(act, gw, gf, act_out, gw_out, gf_out, act_v, gw_v, gf_v, sem):
    def copies(ends, base):
        return [
            pltpu.make_async_copy(src, dst, sem.at[base + i]) for i, (src, dst) in enumerate(ends)
        ]

    reads = copies([(gf, gf_v), (act, act_v), (gw, gw_v)], 0)
    writes = copies([(gf_v, gf_out), (act_v, act_out), (gw_v, gw_out)], 3)
    for copy in reads:
        copy.start()
    for read, write in zip(reads, writes):
        read.wait()
        write.start()
    for copy in writes:
        copy.wait()


def dma(*shape):
    return pltpu.SemaphoreType.DMA(shape)


def on_device(features, weight, tiles, tile_rows, tile_cols, tile_count, cotangent):
    sds = jax.ShapeDtypeStruct
    shapes = (sds((CHUNK, F), bf16), sds((PER, F), f32), sds((PER, PANEL), bf16))
    outs = pl.pallas_call(
        layer_kernel,
        out_shape=shapes,
        in_specs=[any_spec()] * 7,
        out_specs=(any_spec(),) * 3,
        scratch_shapes=[
            *(pltpu.VMEM(x.shape, x.dtype) for x in shapes),
            pltpu.VMEM((F, F), bf16),
            pltpu.VMEM((1, TILE_CAP), i32),
            pltpu.VMEM((1, TILE_CAP), i32),
            pltpu.VMEM((1, 1), i32),
            pltpu.VMEM((CHUNK, F), bf16),
            pltpu.VMEM((TILE_CAP, BLK, BLK), bf16),
            pltpu.VMEM((NROW, PER, PANEL), bf16),
            pltpu.VMEM((BC, BLK, F), bf16),
            pltpu.VMEM((BC, BLK, F), bf16),
            pltpu.VMEM((TILE_CAP, BLK, BLK), bf16),
            pltpu.VMEM((NSUB, NCOL, WIDE * BLK, F), bf16),
            pltpu.VMEM((NSUB, 4, WIDE * BLK, F), bf16),
            pltpu.VMEM((NSUB, 4, 2, WIDE * BLK, F), bf16),
            pltpu.VMEM((NSUB, 4, WIDE * BLK, F), bf16),
            pltpu.VMEM((NSUB, NCOL - 1, WIDE * BLK, F), bf16),
            pltpu.VMEM((BR, F, BLK), bf16),
            pltpu.VMEM((BC, F, BLK), bf16),
            pltpu.VMEM((NROW // 2, 2, PER, PANEL), bf16),
            pltpu.VMEM((2, 8, PER, HALF), bf16),
            pltpu.VMEM((2, 7, PER, HALF), bf16),
            pltpu.VMEM((2, 7, PER, HALF), bf16),
            pltpu.VMEM((2, 8, PER, F), f32),
            pltpu.VMEM((8, PER, F), f32),
            pltpu.VMEM((8, PER, F), f32),
            pltpu.VMEM((7, PER, F), f32),
            pltpu.VMEM((PER, F), f32),
            pltpu.VMEM((NCOL, PER, F), f32),
            pltpu.VMEM((16, TILE_CAP), i32),
            pltpu.SMEM((16, TILE_CAP), i32),
            dma(12), dma(16), dma(16), dma(15), dma(15),
            dma(16, NSUB), dma(16, NSUB), dma(NCOL, NSUB), dma(NCOL, NSUB),
            dma(2), dma(2), dma(2, 7), dma(2, 7), dma(8), dma(8),
            dma(NCOL), dma(NCOL),
        ],
        compiler_params=pltpu.CompilerParams(
            collective_id=0, has_side_effects=True, vmem_limit_bytes=60 * MIB
        ),
        cost_estimate=pl.CostEstimate(
            flops=4 * TILE_CAP * BLK**3, bytes_accessed=11 * MIB, transcendentals=CHUNK * F
        ),
        name="graph_layer",
    )(features.T, weight, tiles, tile_rows[0], tile_cols[0], tile_count, cotangent)
    activated, grad_weight, gf_t = pl.pallas_call(
        write_kernel,
        out_shape=shapes,
        in_specs=[any_spec()] * 3,
        out_specs=(any_spec(),) * 3,
        scratch_shapes=[pltpu.VMEM(x.shape, x.dtype) for x in shapes] + [dma(6)],
        compiler_params=pltpu.CompilerParams(vmem_limit_bytes=60 * MIB),
        name="write_results",
    )(*outs)
    return (activated, grad_weight, gf_t.T)


def solution(mesh):
    return jax.shard_map(
        on_device,
        mesh=mesh,
        in_specs=(
            P("col", "row"),
            P(),
            P("row", "col", None, None, None),
            P("row", "col", None),
            P("row", "col", None),
            P("row", "col"),
            P(("row", "col"), None),
        ),
        out_specs=(P(("row", "col"), None), P("row", None), P("col", "row")),
        check_vma=False,
    )
```

```python
import jax
import jax.numpy as jnp
from jax import lax
from jax.experimental import pallas as pl
from jax.experimental.pallas import tpu as pltpu
from jax.sharding import PartitionSpec as P

F = 128
BLK = 128
NROW = 16
NCOL = 8
BR = 32
BC = 64
TILE_CAP = 256
PANEL = BC * BLK
HALF = PANEL // 2
CHUNK = 512
SUB = CHUNK // BLK
PER = F // NROW
UNROLL = 128
MIB = 1024 * 1024
MESH = pl.DeviceIdType.MESH

f32 = jnp.float32
bf16 = jnp.bfloat16
i32 = jnp.int32

NSUB = 4
WIDE = SUB // NSUB
SUM_PATH = ("yx", "xy", "yx", "xy")
GATHER_PATH = ("xy", "yx", "xy", "yx")
SCHEDULE = "f0 f1 f2 f3 s0 s1 s2 s3 e0 e1 e2 e3 g0 g1 g2 g3"

ORDER, TAKE, KEEP, LAST, HAS = range(5)


def any_spec():
    return pl.BlockSpec(memory_space=pl.ANY)


def start_remote(pending, src, dst, send, recv, **where):
    copy = pltpu.make_async_remote_copy(
        src_ref=src,
        dst_ref=dst,
        send_sem=send,
        recv_sem=recv,
        device_id=where,
        device_id_type=MESH,
    )
    copy.start()
    pending.append(copy)
    return copy


def make_plan(key_block, take, live, dead_block):
    n = TILE_CAP
    across = lax.broadcasted_iota(i32, (n, n), 1)
    down = lax.broadcasted_iota(i32, (n, n), 0)
    block = jnp.where(live, key_block, dead_block)
    block_r = jnp.broadcast_to(block, (n, n))
    block_c = block_r.T
    key_r = block_r * n + across
    key_c = block_c * n + down
    rank = jnp.sum(jnp.where(key_c < key_r, 1, 0), axis=0, keepdims=True)
    rank_c = jnp.broadcast_to(rank, (n, n)).T
    take_c = jnp.broadcast_to(take, (n, n)).T
    hit = rank_c == across
    order = jnp.sum(jnp.where(hit, down, 0), axis=0, keepdims=True)
    taken = jnp.sum(jnp.where(hit, take_c, 0), axis=0, keepdims=True)
    mine = jnp.sum(jnp.where(hit, block_c, 0), axis=0, keepdims=True)
    before = jnp.sum(jnp.where(rank_c == across - 1, block_c, 0), axis=0, keepdims=True)
    first = lax.broadcasted_iota(i32, (1, n), 1) == 0
    keep = jnp.where(first | (mine != before), 0, 1)
    last = jnp.maximum(jnp.sum(jnp.where(block_c <= across, 1, 0), axis=0, keepdims=True) - 1, 0)
    has = jnp.where(jnp.sum(jnp.where(block_c == across, 1, 0), axis=0, keepdims=True) > 0, 1, 0)
    return [order, taken, keep, last, has]


def layer_kernel(
    feat_in, weight_in, tiles, rows_in, cols_in, count_in, cot_in,
    act_out, gw_out, gf_out,
    act, gw, gf, weight, rows_v, cols_v, count_v, cot,
    tv, feat, feat_n, hid, prods, part, x_sum, x_in, y_in, d_in, grad_t,
    back, slabs, pbuf, sbuf, rbuf, gwbuf, gwpair, gwsum, gwrow, gwmine, gwcol, plan_v, plan_s,
    l_sem, a_send, a_recv, f_send, f_recv, r_send, r_recv, g_send, g_recv,
    p_send, p_recv, s_send, s_recv, w_send, w_recv, c_send, c_recv,
):
    me = lax.axis_index("row")
    col = lax.axis_index("col")
    yh = me // 8
    z = (me // 2) % 4
    core = me % 2
    other = 1 - core

    def at(dy, dz, k):
        return ((yh + dy) % 2) * 8 + ((z + dz) % 4) * 2 + k

    partner = at(0, 0, other)
    across = at(1, 0, core)
    peers = [partner] + [at(dy, dz, core) for dy in (0, 1) for dz in range(4) if dy + dz]
    cpeers = [(col + k) % NCOL for k in range(1, NCOL)]

    tile_copy = pltpu.make_async_copy(tiles.at[0, 0], tv, l_sem.at[0])
    tile_copy.start()
    own_copy = pltpu.make_async_copy(feat_in, feat.at[me], l_sem.at[1])
    own_copy.start()
    small = []
    for i, (src, dst) in enumerate(
        [(rows_in, rows_v), (cols_in, cols_v), (count_in, count_v), (weight_in, weight), (cot_in, cot)]
    ):
        copy = pltpu.make_async_copy(src, dst, l_sem.at[3 + i])
        copy.start()
        small.append(copy)

    barrier = pltpu.get_barrier_semaphore()
    for r in peers:
        pl.semaphore_signal(barrier, inc=1, device_id={"row": r}, device_id_type=MESH)
    for c in cpeers:
        pl.semaphore_signal(barrier, inc=1, device_id={"col": c}, device_id_type=MESH)
    pl.semaphore_wait(barrier, len(peers) + len(cpeers))

    pending = []

    def half(ref, h):
        return ref.at[:, pl.ds(h * HALF, HALF)]

    got = {}

    def send(dy, dz, h, ty, tz):
        piece = half(feat.at[at(dy, dz, core)], h)
        src = half(feat_in, h) if (dy, dz) == (0, 0) else piece
        ry, rz = (dy - ty) % 2, (dz - tz) % 4
        index = h * 8 + ry * 4 + rz
        got[ry, rz, h] = start_remote(
            pending, src, piece, a_send.at[index], a_recv.at[index], row=at(ty, tz, core)
        )

    for tz in (2, 1, 3):
        send(0, 0, 0, 0, tz)
    send(0, 0, 1, 1, 0)
    for tz in (2, 1, 3):
        send(0, 0, 1, 0, tz)
    send(0, 0, 0, 1, 0)
    own_hand = start_remote(
        pending, feat_in, feat.at[me], f_send.at[0], f_recv.at[0], row=partner
    )

    for copy in small:
        copy.wait()
    live = lax.broadcasted_iota(i32, (1, TILE_CAP), 1) < count_v[0, 0]
    forward = make_plan(rows_v[...], cols_v[...], live, BR)
    backward = make_plan(cols_v[...], rows_v[...], live, BC)
    for i, line in enumerate(forward + backward):
        plan_v[i : i + 1, :] = line
    plan_copy = pltpu.make_async_copy(plan_v, plan_s, l_sem.at[2])
    plan_copy.start()

    handed = [own_hand]

    def hand(dy, dz, h):
        index = len(handed)
        piece = half(feat.at[at(dy, dz, core)], h)
        handed.append(
            start_remote(
                pending, piece, piece, f_send.at[index], f_recv.at[index], row=partner
            )
        )

    got[1, 0, 1].wait_recv()
    for tz in (2, 1, 3):
        send(1, 0, 1, 0, tz)
    hand(1, 0, 1)
    for dz in (1, 3, 2):
        got[0, dz, 0].wait_recv()
        send(0, dz, 0, 1, 0)
        hand(0, dz, 0)
    for dy, dz, h in (
        (1, 0, 0), (0, 1, 1), (0, 3, 1), (0, 2, 1), (1, 1, 0), (1, 3, 0), (1, 2, 0),
        (1, 1, 1), (1, 3, 1), (1, 2, 1),
    ):
        got[dy, dz, h].wait_recv()
        hand(dy, dz, h)
    own_copy.wait()
    for copy in handed:
        copy.wait_recv()

    w = weight[...]

    def hidden_step(i, carry):
        for t in range(16):
            b = i * 16 + t
            span = pl.ds(pl.multiple_of(b * BLK, BLK), BLK)
            nodes = feat[:, :, span].astype(f32).reshape(F, BLK).T.astype(bf16)
            feat_n[b] = nodes
            hid[b] = jnp.dot(nodes, w, preferred_element_type=f32).astype(bf16)
        return carry

    lax.fori_loop(0, BC // 16, hidden_step, 0)

    plan_copy.wait()
    tile_copy.wait()

    def forward_step(i, total):
        for t in range(UNROLL):
            p = i * UNROLL + t
            keep = plan_s[KEEP, p].astype(f32)
            total = total * keep + jnp.dot(
                tv[plan_s[ORDER, p]], hid[plan_s[TAKE, p]], preferred_element_type=f32
            )
            prods[p] = total.astype(bf16)
        return total

    lax.fori_loop(0, TILE_CAP // UNROLL, forward_step, jnp.zeros((BLK, F), f32))
    for b in range(BR):
        has = plan_s[HAS, b].astype(f32)
        sub, place = b % SUB // WIDE, b % SUB % WIDE * BLK
        block = (prods[plan_s[LAST, b]].astype(f32) * has).astype(bf16)
        part[sub, b // SUB, place : place + BLK] = block

    x = col // 2
    yl = col % 2

    def spot(dx, dy):
        return ((x + dx) % 4) * 2 + (yl + dy) % 2

    def both(q, dx):
        return part.at[q, pl.ds(((x + dx) % 4) * 2, 2)]

    def add_to(src, dst, q, index, to):
        return start_remote(
            pending, src, dst, r_send.at[index, q], r_recv.at[index, q], col=to
        )

    x_got = {}
    y_got = {}
    every = [(2, 1), (2, 0), (1, 1), (3, 1), (1, 0), (3, 0), (0, 1)]
    def first(q):
        if SUM_PATH[q] == "yx":
            for dx in (2, 1, 3, 0):
                src = part.at[q, spot(dx, 1)]
                y_got[q, dx] = add_to(src, y_in.at[q, dx], q, 4 + dx, spot(0, 1))
        elif SUM_PATH[q] == "xy":
            for dx in (2, 1, 3):
                x_got[q, dx] = add_to(both(q, dx), x_in.at[q, dx], q, dx, spot(dx, 0))
        else:
            for k, (dx, dy) in enumerate(every):
                src = part.at[q, spot(dx, dy)]
                x_got[q, k] = add_to(src, d_in.at[q, k], q, 8 + k, spot(dx, dy))

    def second(q):
        if SUM_PATH[q] == "yx":
            for dx in (2, 1, 3):
                y_got[q, dx].wait_recv()
                x_sum[q, dx] = (
                    part[q, spot(dx, 0)].astype(f32) + y_in[q, dx].astype(f32)
                ).astype(bf16)
                x_got[q, dx] = add_to(x_sum.at[q, dx], x_in.at[q, dx, 0], q, dx, spot(dx, 0))
        elif SUM_PATH[q] == "xy":
            side = part[q, spot(0, 1)].astype(f32)
            for dx in (2, 1, 3):
                x_got[q, dx].wait_recv()
                side = side + x_in[q, dx, (yl + 1) % 2].astype(f32)
            x_sum[q, 0] = side.astype(bf16)
            y_got[q, 0] = add_to(x_sum.at[q, 0], y_in.at[q, 0], q, 4, spot(0, 1))

    def summed(q):
        pre = part[q, col].astype(f32)
        if SUM_PATH[q] == "direct":
            for k in range(NCOL - 1):
                x_got[q, k].wait_recv()
                pre = pre + d_in[q, k].astype(f32)
            return pre
        for dx in (2, 1, 3):
            if SUM_PATH[q] == "yx":
                x_got[q, dx].wait_recv()
                pre = pre + x_in[q, dx, 0].astype(f32)
            else:
                pre = pre + x_in[q, dx, yl].astype(f32)
        y_got[q, 0].wait_recv()
        return pre + y_in[q, 0].astype(f32)

    gathers = {}

    def gather(dx, dy, q, tx, ty):
        piece = grad_t.at[pl.ds(spot(dx, dy) * SUB + q * WIDE, WIDE)]
        rx, ry = (dx - tx) % 4, (dy - ty) % 2
        index = rx * 2 + ry
        gathers[rx, ry, q] = start_remote(
            pending, piece, piece, g_send.at[index, q], g_recv.at[index, q], col=spot(tx, ty)
        )

    def here(dx, dy, q):
        gathers.pop((dx, dy, q)).wait_recv()

    def finish(q):
        pre = summed(q)
        sig = jax.nn.sigmoid(pre)
        span = pl.ds(q * WIDE * BLK, WIDE * BLK)
        grad = cot[span].astype(f32) * sig * (1.0 + pre * (1.0 - sig))
        for i in range(WIDE):
            block = grad[i * BLK : (i + 1) * BLK].T
            grad_t[col * SUB + q * WIDE + i] = block.astype(bf16)
        if GATHER_PATH[q] == "yx":
            ways = [(0, 1), (2, 0), (1, 0), (3, 0)]
        elif GATHER_PATH[q] == "xy":
            ways = [(2, 0), (1, 0), (3, 0), (0, 1)]
        else:
            ways = every
        for tx, ty in ways:
            gather(0, 0, q, tx, ty)
        act[span] = (pre * sig).astype(bf16)

    def spread(q):
        if GATHER_PATH[q] == "yx":
            here(0, 1, q)
            for tx in (2, 1, 3):
                gather(0, 1, q, tx, 0)
        elif GATHER_PATH[q] == "xy":
            for dx in (3, 1, 2):
                here(dx, 0, q)
                gather(dx, 0, q, 0, 1)

    def drain(q):
        got = [v for d in (x_got, y_got) for key, v in d.items() if key[0] == q]
        for copy in got:
            copy.wait_send()
            pending[:] = [other_copy for other_copy in pending if other_copy is not copy]

    steps = {"f": first, "s": second, "e": finish, "g": spread, "d": drain}
    for step in SCHEDULE.split():
        steps[step[0]](int(step[1]))
    act_copy = pltpu.make_async_copy(act, act_out, l_sem.at[8])
    act_copy.start()
    for key in list(gathers):
        here(*key)

    def backward_step(i, total):
        for t in range(UNROLL):
            p = i * UNROLL + t
            keep = plan_s[5 + KEEP, p].astype(f32)
            total = total * keep + jnp.dot(
                grad_t[plan_s[5 + TAKE, p]], tv[plan_s[5 + ORDER, p]], preferred_element_type=f32
            )
            prods[p] = total.astype(bf16)
        return total

    lax.fori_loop(0, TILE_CAP // UNROLL, backward_step, jnp.zeros((F, BLK), f32))

    chips = [(0, 1), (0, 2), (0, 3), (1, 0), (1, 1), (1, 2), (1, 3), (0, 0)]
    pairs = {}

    def panel_step(i, total):
        for t in range(16):
            b = i * 16 + t
            has = plan_s[5 + HAS, b].astype(f32)
            block = (prods[plan_s[5 + LAST, b]].astype(f32) * has).astype(bf16)
            back[b] = block
            out = jnp.dot(w, block, preferred_element_type=f32)
            span = pl.ds(pl.multiple_of(b * BLK, BLK), BLK)
            slabs[:, :, :, span] = out.reshape(NROW // 2, 2, PER, BLK).astype(bf16)
            total = total + jnp.dot(block, feat_n[b], preferred_element_type=f32)
        return total

    def start_pairs(h):
        pairs[h] = start_remote(
            pending,
            slabs.at[:, other, :, pl.ds(h * HALF, HALF)],
            pbuf.at[h],
            p_send.at[h],
            p_recv.at[h],
            row=partner,
        )

    gw_part = lax.fori_loop(0, BC // 32, panel_step, jnp.zeros((F, F), f32))
    start_pairs(0)
    gw_part = lax.fori_loop(BC // 32, BC // 16, panel_step, gw_part)
    gw_part = gw_part.T
    for r in range(NROW):
        gwbuf[r % 2, r // 2] = gw_part[r * PER : (r + 1) * PER]
    gw_pair = start_remote(
        pending, gwbuf.at[other], gwpair, w_send.at[7], w_recv.at[7], row=partner
    )


    def pair_sum(dy, dz, h):
        if h in pairs:
            pairs.pop(h).wait_recv()
        chip = ((yh + dy) % 2) * 4 + (z + dz) % 4
        own = slabs[chip, core, :, h * HALF : (h + 1) * HALF]
        return own.astype(f32) + pbuf[h, chip].astype(f32)

    def pass_sum(value, h, k, to):
        sbuf[h, k] = value.astype(bf16)
        return start_remote(
            pending, sbuf.at[h, k], rbuf.at[h, k], s_send.at[h, k], s_recv.at[h, k], row=to
        )

    start_pairs(1)

    gw_pair.wait_recv()
    gwsum[...] = gwbuf[core] + gwpair[...]
    shares = []
    for k, (dy, dz) in enumerate(chips[:7]):
        chip = ((yh + dy) % 2) * 4 + (z + dz) % 4
        shares.append(
            start_remote(
                pending,
                gwsum.at[chip],
                gwrow.at[k],
                w_send.at[k],
                w_recv.at[k],
                row=at(dy, dz, core),
            )
        )

    sums = {}
    for dz in (2, 1, 3):
        for dy in (1, 0):
            k = chips.index((dy, dz))
            sums[dy, dz, 0] = pass_sum(pair_sum(dy, dz, 0), 0, k, at(0, dz, core))
    for dz in (2, 1, 3, 0):
        k = chips.index((1, dz))
        sums[1, dz, 1] = pass_sum(pair_sum(1, dz, 1), 1, k, across)

    gw_sum = gwsum[me // 2]
    for k in range(7):
        shares[k].wait_recv()
        gw_sum = gw_sum + gwrow[k]
    gwmine[...] = gw_sum
    spreads = []
    for k in range(1, NCOL):
        spreads.append(
            start_remote(
                pending, gwmine, gwcol.at[k], c_send.at[k], c_recv.at[k], col=cpeers[k - 1]
            )
        )

    for dz in (2, 1, 3):
        k = chips.index((0, dz))
        value = pair_sum(0, dz, 1)
        sums[1, dz, 1].wait_recv()
        value = value + rbuf[1, chips.index((1, dz))].astype(f32)
        sums[0, dz, 1] = pass_sum(value, 1, k, at(0, dz, core))

    value = pair_sum(1, 0, 0)
    for dz in (1, 2, 3):
        sums[1, dz, 0].wait_recv()
        value = value + rbuf[0, chips.index((1, dz))].astype(f32)
    sums[1, 0, 0] = pass_sum(value, 0, chips.index((1, 0)), across)

    total = pair_sum(0, 0, 1)
    sums[1, 0, 1].wait_recv()
    total = total + rbuf[1, chips.index((1, 0))].astype(f32)
    for dz in (1, 2, 3):
        sums[0, dz, 1].wait_recv()
        total = total + rbuf[1, chips.index((0, dz))].astype(f32)
    gf[:, HALF:] = total.astype(bf16)
    outs = [act_copy, pltpu.make_async_copy(half(gf, 1), half(gf_out, 1), l_sem.at[9])]
    outs[1].start()

    total = pair_sum(0, 0, 0)
    for dy, dz in ((0, 1), (0, 2), (0, 3), (1, 0)):
        sums[dy, dz, 0].wait_recv()
        total = total + rbuf[0, chips.index((dy, dz))].astype(f32)
    gf[:, :HALF] = total.astype(bf16)
    outs.append(pltpu.make_async_copy(half(gf, 0), half(gf_out, 0), l_sem.at[10]))
    outs[2].start()

    for k in range(1, NCOL):
        spreads[k - 1].wait_recv()
        gw_sum = gw_sum + gwcol[k]
    gw[...] = gw_sum
    outs.append(pltpu.make_async_copy(gw, gw_out, l_sem.at[11]))
    outs[3].start()
    for copy in pending:
        copy.wait_send()
    for copy in outs:
        copy.wait()


def write_kernel(act, gw, gf, act_out, gw_out, gf_out, act_v, gw_v, gf_v, sem):
    def copies(ends, base):
        return [
            pltpu.make_async_copy(src, dst, sem.at[base + i]) for i, (src, dst) in enumerate(ends)
        ]

    reads = copies([(gf, gf_v), (act, act_v), (gw, gw_v)], 0)
    writes = copies([(gf_v, gf_out), (act_v, act_out), (gw_v, gw_out)], 3)
    for copy in reads:
        copy.start()
    for read, write in zip(reads, writes):
        read.wait()
        write.start()
    for copy in writes:
        copy.wait()


def dma(*shape):
    return pltpu.SemaphoreType.DMA(shape)


def on_device(features, weight, tiles, tile_rows, tile_cols, tile_count, cotangent):
    sds = jax.ShapeDtypeStruct
    shapes = (sds((CHUNK, F), bf16), sds((PER, F), f32), sds((PER, PANEL), bf16))
    outs = pl.pallas_call(
        layer_kernel,
        out_shape=shapes,
        in_specs=[any_spec()] * 7,
        out_specs=(any_spec(),) * 3,
        scratch_shapes=[
            *(pltpu.VMEM(x.shape, x.dtype) for x in shapes),
            pltpu.VMEM((F, F), bf16),
            pltpu.VMEM((1, TILE_CAP), i32),
            pltpu.VMEM((1, TILE_CAP), i32),
            pltpu.VMEM((1, 1), i32),
            pltpu.VMEM((CHUNK, F), bf16),
            pltpu.VMEM((TILE_CAP, BLK, BLK), bf16),
            pltpu.VMEM((NROW, PER, PANEL), bf16),
            pltpu.VMEM((BC, BLK, F), bf16),
            pltpu.VMEM((BC, BLK, F), bf16),
            pltpu.VMEM((TILE_CAP, BLK, BLK), bf16),
            pltpu.VMEM((NSUB, NCOL, WIDE * BLK, F), bf16),
            pltpu.VMEM((NSUB, 4, WIDE * BLK, F), bf16),
            pltpu.VMEM((NSUB, 4, 2, WIDE * BLK, F), bf16),
            pltpu.VMEM((NSUB, 4, WIDE * BLK, F), bf16),
            pltpu.VMEM((NSUB, NCOL - 1, WIDE * BLK, F), bf16),
            pltpu.VMEM((BR, F, BLK), bf16),
            pltpu.VMEM((BC, F, BLK), bf16),
            pltpu.VMEM((NROW // 2, 2, PER, PANEL), bf16),
            pltpu.VMEM((2, 8, PER, HALF), bf16),
            pltpu.VMEM((2, 7, PER, HALF), bf16),
            pltpu.VMEM((2, 7, PER, HALF), bf16),
            pltpu.VMEM((2, 8, PER, F), f32),
            pltpu.VMEM((8, PER, F), f32),
            pltpu.VMEM((8, PER, F), f32),
            pltpu.VMEM((7, PER, F), f32),
            pltpu.VMEM((PER, F), f32),
            pltpu.VMEM((NCOL, PER, F), f32),
            pltpu.VMEM((16, TILE_CAP), i32),
            pltpu.SMEM((16, TILE_CAP), i32),
            dma(12), dma(16), dma(16), dma(15), dma(15),
            dma(16, NSUB), dma(16, NSUB), dma(NCOL, NSUB), dma(NCOL, NSUB),
            dma(2), dma(2), dma(2, 7), dma(2, 7), dma(8), dma(8),
            dma(NCOL), dma(NCOL),
        ],
        compiler_params=pltpu.CompilerParams(
            collective_id=0, has_side_effects=True, vmem_limit_bytes=60 * MIB
        ),
        cost_estimate=pl.CostEstimate(
            flops=4 * TILE_CAP * BLK**3, bytes_accessed=11 * MIB, transcendentals=CHUNK * F
        ),
        name="graph_layer",
    )(features.T, weight, tiles, tile_rows[0], tile_cols[0], tile_count, cotangent)
    activated, grad_weight, gf_t = pl.pallas_call(
        write_kernel,
        out_shape=shapes,
        in_specs=[any_spec()] * 3,
        out_specs=(any_spec(),) * 3,
        scratch_shapes=[pltpu.VMEM(x.shape, x.dtype) for x in shapes] + [dma(6)],
        compiler_params=pltpu.CompilerParams(vmem_limit_bytes=60 * MIB),
        name="write_results",
    )(*outs)
    return (activated, grad_weight, gf_t.T)


def solution(mesh):
    return jax.shard_map(
        on_device,
        mesh=mesh,
        in_specs=(
            P("col", "row"),
            P(),
            P("row", "col", None, None, None),
            P("row", "col", None),
            P("row", "col", None),
            P("row", "col"),
            P(("row", "col"), None),
        ),
        out_specs=(P(("row", "col"), None), P("row", None), P("col", "row")),
        check_vma=False,
    )
```
